512 devices in a mesh: member: 8 (over z_hi, y), band: 64 (over x, z_lo, core).
Axes of the slice: x: 4, y: 4, z: 16 (z_hi: 2, z_lo: 8; z = z_hi * 8 + z_lo), core: 2. Of those that a mesh axis runs over, the one named last changes fastest.
Arguments:
- mesh_latent: bfloat16 [8, 8192, 512], P('member', 'band'), may hold values from -6 to 6
- grid_latent: bfloat16 [8, 20480, 512], P('member', 'band'), may hold values from -16 to 16
- senders: int32 [20480, 3], P('band'), may hold values from 0 to 191, as said below
- live_points: int32 [64], replicated, may hold values from 80 to 320, as said below
- target: bfloat16 [100, 20480], P(None, 'band'), may hold values from -6 to 6
- w_send: bfloat16 [512, 512], replicated, may hold values from -0.25 to 0.25
- w_recv: bfloat16 [512, 512], replicated, may hold values from -0.25 to 0.25
- w_edge: bfloat16 [512, 512], replicated, may hold values from -0.25 to 0.25
- w_out: bfloat16 [512, 100], replicated, may hold values from -0.25 to 0.25
- gain: float32 [512], replicated, may hold values from 0.5 to 1.5
Outputs:
- crps_field: float32 [20480], P('band')
- grad_send: float32 [512, 512], P('band')
- grad_recv: float32 [512, 512], P('band')
- grad_edge: float32 [512, 512], P('band')
- grad_out: float32 [512, 100], P('band')
The draws below stay inside these ranges and needn't reach their ends.
Inputs may be any that keep to these rules, and one draw needn't show every extreme that they name: `senders`: index into the band's 128 own mesh rows extended by 32 rows of each neighbouring band (index 32 is the band's first own row; rows beyond the poles are zero). `live_points`: positions at or past a band's count are padding.
All inputs are finite; a program needn't handle non-finite values.
Results may differ from the reference program's by a relative error of at most 0.012.
Values may be sent and summed in bfloat16 or wider, within the bound.
A program may use at most 64 MiB of HBM per device.

```python
import jax
import jax.numpy as jnp
from jax import lax

D = 512
VARS = 100
K = 3
HALO = 32
P_DEV = 320
Q_DEV = 128
MEMBERS = 8
NBANDS = 64
POINTS = 20480
MESH = 8192


def draw_senders(key, part):
    key = jax.random.fold_in(key, 11)
    local = jnp.arange(POINTS, dtype=jnp.int32) % P_DEV
    center = HALO + local * Q_DEV // P_DEV
    offsets = jax.random.randint(key, (POINTS, K), -HALO, HALO + 1)
    picked = jnp.clip(center[:, None] + offsets, 0, Q_DEV + 2 * HALO - 1)
    column = jnp.arange(K, dtype=jnp.int32)[None, :]
    picked = jnp.where((local[:, None] == 0) & (column == 0), 0, picked)
    picked = jnp.where((local[:, None] == P_DEV - 1) & (column == 0), Q_DEV + 2 * HALO - 1, picked)
    return picked.astype(jnp.int32)


def draw_live_points(key, part):
    key = jax.random.fold_in(key, 12)
    rows = jnp.arange(NBANDS, dtype=jnp.int32)
    halfway = max(NBANDS // 2, 1)
    distance = jnp.minimum(rows, NBANDS - 1 - rows)
    base = P_DEV // 4 + 3 * P_DEV // 4 * distance // halfway
    jitter = jax.random.randint(key, (NBANDS,), 0, P_DEV // 8 + 1) * (rows != 0).astype(jnp.int32)
    counts = jnp.minimum(base + jitter, P_DEV)
    counts = jnp.where(rows == NBANDS // 2, P_DEV, counts)
    return counts.astype(jnp.int32)


def raised(result, rng, source, target, blocks, factor):
    owner, partner = [(jnp.arange(result.shape[position]) // (result.shape[position] // blocks)).reshape([-1 if axis == position else 1 for axis in range(result.ndim)]) for position in (source, target)]
    chosen = jax.random.permutation(rng, blocks)[partner]
    strong = (owner == chosen) | (owner == (partner + blocks // 2) % blocks)
    return jnp.where(strong, factor * result, result)


def steps_of(stream_key, shape, shards, least, high):
    level, own = 1.0, jax.random.fold_in(stream_key, 6)
    for axis_at, shards_of in shards:
        draws = jnp.exp(jax.random.uniform(jax.random.fold_in(own, axis_at), (shards_of,), jnp.float32, least / len(shards), high / len(shards)))
        level = level * jnp.repeat(draws, shape[axis_at] // shards_of).reshape([-1 if axis == axis_at else 1 for axis in range(len(shape))])
    return level


def bell_draw(stream_key, extent, scale, most, shards=(), kind=jnp.bfloat16):
    drawn = scale * jax.random.normal(stream_key, extent, jnp.float32)
    if shards:
        drawn = drawn * steps_of(stream_key, extent, shards, -0.22, 0.18)
    return jnp.clip(drawn, -most, most).astype(kind)


def heavy_noise(own_key, shape, deviation, bound, shards, heavy, held_as=jnp.bfloat16):
    drawn = deviation * jax.random.normal(own_key, shape, jnp.float32)
    if shards:
        drawn = drawn * steps_of(own_key, shape, shards, -0.22, 0.18)
    return jnp.clip(raised(drawn, jax.random.fold_in(own_key, 3), *heavy), -bound, bound).astype(held_as)


def setup_inputs(seed: int = 0) -> dict:
    arg_keys = jax.random.split(jax.random.key(seed), 11)
    mesh_latent = bell_draw(arg_keys[0], (MEMBERS, MESH, D), 1.0, 6.0, ((0, 8), (1, 64)))
    grid_latent = heavy_noise(arg_keys[1], (MEMBERS, POINTS, D), 1.0, 16.0, ((0, 8), (1, 64)), (1, 2, 64, 4.0))
    senders = draw_senders(jax.random.fold_in(arg_keys[10], 71), 0)
    live_points = draw_live_points(jax.random.fold_in(arg_keys[10], 71), 0)
    target = bell_draw(arg_keys[4], (VARS, POINTS), 1.0, 6.0, ((1, 64),))
    w_send = bell_draw(arg_keys[5], (D, D), D ** -0.5, 0.25)
    w_recv = bell_draw(arg_keys[6], (D, D), D ** -0.5, 0.25)
    w_edge = bell_draw(arg_keys[7], (D, D), D ** -0.5, 0.25)
    w_out = bell_draw(arg_keys[8], (D, VARS), D ** -0.5, 0.25)
    gain = jnp.clip(1.0 + 0.1 * jax.random.normal(arg_keys[9], (D,), jnp.float32), 0.5, 1.5)
    return dict(mesh_latent=mesh_latent, grid_latent=grid_latent, senders=senders, live_points=live_points, target=target, w_send=w_send, w_recv=w_recv, w_edge=w_edge, w_out=w_out, gain=gain)


smooth_sq = 0.0625

def decode_band(grid_rows, mesh_rows, sender_rows, w_send, w_recv, w_edge, w_out, gain):
    sent_rows = jnp.dot(mesh_rows, w_send, preferred_element_type=jnp.float32)
    recv_rows = jnp.dot(grid_rows, w_recv, preferred_element_type=jnp.float32)
    preact = jnp.take(sent_rows, sender_rows, axis=0) + recv_rows[:, None, :]
    agg_in = lax.optimization_barrier(jnp.sum(jax.nn.silu(preact), axis=1)).astype(jnp.bfloat16)
    hidden_sum = grid_rows.astype(jnp.float32) + jnp.dot(agg_in, w_edge, preferred_element_type=jnp.float32)
    inv_rms = lax.rsqrt(lax.optimization_barrier(jnp.mean(hidden_sum * hidden_sum, axis=1, keepdims=True)) + 1e-05)
    normed = (hidden_sum * inv_rms * gain).astype(jnp.bfloat16)
    pred = lax.dot_general(w_out, normed, (((0,), (1,)), ((), ())), preferred_element_type=jnp.float32)
    return (pred.astype(jnp.bfloat16), (preact, agg_in, hidden_sum, inv_rms, normed))

def backward_band(field_grad, grid_rows, mesh_rows, sender_rows, saved, w_edge, w_out, gain):
    preact, agg_in, hidden_sum, inv_rms, normed = saved
    grad16 = field_grad.astype(jnp.bfloat16)
    d_out = lax.dot_general(normed, grad16, (((0,), (1,)), ((), ())), preferred_element_type=jnp.float32)
    d_normed = lax.dot_general(grad16, w_out, (((0,), (1,)), ((), ())), preferred_element_type=jnp.float32)
    gained = d_normed * gain
    d_hidden = inv_rms * gained - hidden_sum * inv_rms ** 3 * lax.optimization_barrier(jnp.mean(gained * hidden_sum, axis=1, keepdims=True))
    d_hidden = d_hidden.astype(jnp.bfloat16)
    d_edge = lax.dot_general(agg_in, d_hidden, (((0,), (0,)), ((), ())), preferred_element_type=jnp.float32)
    d_aggin = lax.dot_general(d_hidden, w_edge, (((1,), (1,)), ((), ())), preferred_element_type=jnp.float32)
    sigmoid_v = jax.nn.sigmoid(preact)
    d_preact = d_aggin[:, None, :] * sigmoid_v * (1.0 + preact * (1.0 - sigmoid_v))
    d_recv = lax.optimization_barrier(jnp.sum(d_preact, axis=1)).astype(jnp.bfloat16)
    d_recvw = lax.dot_general(grid_rows, d_recv, (((0,), (0,)), ((), ())), preferred_element_type=jnp.float32)
    width = d_preact.shape[2]
    d_sent = jax.ops.segment_sum(d_preact.reshape(-1, width), sender_rows.reshape(-1), num_segments=mesh_rows.shape[0])
    d_sent = d_sent.astype(jnp.bfloat16)
    d_sendw = lax.dot_general(mesh_rows, d_sent, (((0,), (0,)), ((), ())), preferred_element_type=jnp.float32)
    return (d_sendw, d_recvw, d_edge, d_out)

def pair_terms(fields, target, live_mask, scale):
    count = fields.shape[0]
    values = fields.astype(jnp.float32)
    truth = target.astype(jnp.float32)
    error = values - truth
    root_error = jnp.sqrt(error * error + smooth_sq)
    abs_error = lax.optimization_barrier(jnp.sum(root_error, axis=0)) / count
    spread = jnp.zeros(truth.shape, jnp.float32)
    pair_slope = jnp.zeros(values.shape, jnp.float32)
    for other in range(count):
        differ = values - values[other]
        root_differ = jnp.sqrt(differ * differ + smooth_sq)
        spread = spread + lax.optimization_barrier(jnp.sum(root_differ, axis=0))
        pair_slope = pair_slope + differ / root_differ
    crps = lax.optimization_barrier(jnp.sum(abs_error - spread / (2.0 * count * (count - 1)), axis=0)) * live_mask
    field_grad = (error / root_error / count - pair_slope / (count * (count - 1))) * (live_mask * scale)
    return (crps, field_grad)

def reference(mesh_latent, grid_latent, senders, live_points, target, w_send, w_recv, w_edge, w_out, gain):
    zero_rows = jnp.zeros((MEMBERS, HALO, D), jnp.bfloat16)
    padded = jnp.concatenate([zero_rows, mesh_latent, zero_rows], axis=1)
    band_ids = jnp.arange(NBANDS, dtype=jnp.int32)

    def inputs(member, band_id):
        grid_rows = lax.dynamic_slice_in_dim(grid_latent[member], band_id * P_DEV, P_DEV, 0)
        mesh_rows = lax.dynamic_slice_in_dim(padded[member], band_id * Q_DEV, Q_DEV + 2 * HALO, 0)
        sender_rows = lax.dynamic_slice_in_dim(senders, band_id * P_DEV, P_DEV, 0)
        return (grid_rows, mesh_rows, sender_rows)
    preds = []
    for member in range(MEMBERS):

        def forward_one(band_id):
            grid_rows, mesh_rows, sender_rows = inputs(member, band_id)
            return decode_band(grid_rows, mesh_rows, sender_rows, w_send, w_recv, w_edge, w_out, gain)[0]
        stacked = lax.map(forward_one, band_ids)
        preds.append(jnp.transpose(stacked, (1, 0, 2)).reshape(VARS, POINTS))
    fields = jnp.stack(preds)
    positions = jnp.arange(P_DEV, dtype=jnp.int32)
    live_mask = (positions[None, :] < live_points[:, None]).astype(jnp.float32).reshape(POINTS)
    scale = 1.0 / (jnp.sum(live_points).astype(jnp.float32) * VARS)
    crps_field, field_grad = pair_terms(fields, target, live_mask, scale)
    totals = None
    for member in range(MEMBERS):

        def backward_one(band_id):
            grid_rows, mesh_rows, sender_rows = inputs(member, band_id)
            saved = decode_band(grid_rows, mesh_rows, sender_rows, w_send, w_recv, w_edge, w_out, gain)[1]
            band_grad = lax.dynamic_slice_in_dim(field_grad[member], band_id * P_DEV, P_DEV, 1)
            return backward_band(band_grad, grid_rows, mesh_rows, sender_rows, saved, w_edge, w_out, gain)
        parts = lax.map(backward_one, band_ids)
        summed = tuple((lax.optimization_barrier(jnp.sum(piece, axis=0)) for piece in parts))
        totals = summed if totals is None else tuple((a + b for a, b in zip(totals, summed)))
    return (crps_field, totals[0], totals[1], totals[2], totals[3])
```

```python
import jax
import jax.numpy as jnp
from jax import lax
from jax.experimental import pallas as pl
from jax.experimental.pallas import tpu as pltpu
from jax.sharding import PartitionSpec as P

HALO = 32
SMOOTH_SQ = 0.0625
MESH = pl.DeviceIdType.MESH
F32 = jnp.float32
BF16 = jnp.bfloat16

D = 512
VARS = 100
PTS = 320
OWN = 128
ROWS = OWN + 2 * HALO
PACK = 256
TAIL = PTS - PACK
FOLD = 25


def dot(a, b, dims=((1,), (0,))):
    return lax.dot_general(a, b, (dims, ((), ())), preferred_element_type=F32)


def lanes_of(shape):
    return lax.broadcasted_iota(jnp.int32, shape, 1)


def rows_of(shape):
    return lax.broadcasted_iota(jnp.int32, shape, 0)


def pack_field(x):
    tail = x[PACK:]
    lane = lanes_of(tail.shape)
    inside = (lane >= VARS) & (lane < VARS + FOLD)
    parts = [jnp.where(inside, pltpu.roll(tail, VARS - FOLD * j, 1), 0.0) for j in range(4)]
    return x[:PACK] + jnp.concatenate(parts, axis=0)


def unpack_field(x):
    lane = lanes_of((TAIL, 128))
    tail = jnp.zeros((TAIL, 128), F32)
    for j in range(4):
        moved = pltpu.roll(x[TAIL * j : TAIL * (j + 1)], 128 - (VARS - FOLD * j), 1)
        tail = tail + jnp.where((lane >= FOLD * j) & (lane < FOLD * (j + 1)), moved, 0.0)
    main = jnp.where(lanes_of((PACK, 128)) < VARS, x, 0.0)
    return jnp.concatenate([main, tail], axis=0)


def kernel(
    mesh_ref, grid_ref, send_ref, live_ref, target_ref, ws_ref, wr_ref, we_ref, wo_ref, gain_ref,
    crps_out, gs_out, gr_out, ge_out, go_out,
    halo, wo, tpad, spad, onehot_t, slope_k, fields, crow, crow_z,
    part, core_in, summed, x_in1, x_sum1, y_in1, y_in2, y_sum2, x_in2, slab, z_in, final,
    s_halo, r_halo, s_fz, r_fz, s_fy, r_fy, s_fzy, r_fzy, s_cy, r_cy, s_cz, r_cz,
    s_core, r_core, s_x1, r_x1, s_y1, r_y1, s_y2, r_y2, s_x2, r_x2, s_z, r_z, s_g, r_g,
):
    member = lax.axis_index("member")
    band = lax.axis_index("band")
    zh, y = member // 4, member % 4
    x, zl, c = band // 16, (band // 2) % 8, band % 2
    z = zh * 8 + zl

    def dev(z_, y_, x_, c_):
        return ((z_ // 8) * 4 + y_, x_ * 16 + (z_ % 8) * 2 + c_)

    def z_peer(k):
        return dev((z + k) % 16, y, x, c)

    def y_peer(k):
        return dev(z, (y + k) % 4, x, c)

    def x_peer(k):
        return dev(z, y, (x + k) % 4, c)

    sibling = dev(z, y, x, 1 - c)
    upper = (member, (band + 1) % 64)
    lower = (member, (band + 63) % 64)
    other = (member, (band + 2 * c - 1 + 64) % 64)

    def rcopy(src, dst, ss, rs, to):
        return pltpu.make_async_remote_copy(
            src_ref=src, dst_ref=dst, send_sem=ss, recv_sem=rs, device_id=to, device_id_type=MESH
        )

    barrier = pltpu.get_barrier_semaphore()
    peers = [z_peer(k) for k in range(1, 16)]
    peers += [y_peer(k) for k in (1, 2, 3)] + [x_peer(k) for k in (1, 2, 3)]
    peers += [sibling, other]
    for p in peers:
        pl.semaphore_signal(barrier, inc=1, device_id=p, device_id_type=MESH)

    sent_own = dot(mesh_ref[...], ws_ref[...])
    recv_rows = dot(grid_ref[...], wr_ref[...])
    wo[...] = jnp.zeros(wo.shape, BF16)
    wo[:, :VARS] = wo_ref[...]
    tpad[...] = jnp.zeros(tpad.shape, F32)
    tpad[:VARS, :PTS] = target_ref[...].astype(F32)
    truth = pack_field(jnp.transpose(tpad[...])[:PTS])
    spad[...] = jnp.zeros(spad.shape, F32)
    spad[:PTS, :3] = send_ref[...].astype(F32)
    senders_t = jnp.transpose(spad[...])[:8, :PTS].astype(jnp.int32)

    def moved(s):
        return jnp.where(s < HALO, s + OWN, jnp.where(s < HALO + OWN, s - HALO, s))

    index = moved(send_ref[...])
    index_t = moved(senders_t)
    for k in range(3):
        hit = rows_of((ROWS, PTS)) == index_t[k : k + 1, :]
        onehot_t[k] = jnp.where(hit, 1.0, 0.0).astype(BF16)
    live = live_ref[...]
    lane64 = lanes_of(live.shape)
    count = jnp.sum(jnp.where(lane64 == band, live, 0).astype(F32), axis=1, keepdims=True)
    total = jnp.sum(live.astype(F32), axis=1, keepdims=True)
    scale = 1.0 / (total * VARS)
    row = rows_of((PACK, 128))
    lane = lanes_of((PACK, 128))
    point = jnp.where(lane < VARS, row, PACK + row % TAIL)
    mask = jnp.where((lane < VARS + FOLD) & (point.astype(F32) < count), 1.0, 0.0)

    pl.semaphore_wait(barrier, len(peers))

    halo_copies = []
    for i in range(2):
        for j in range(4):
            cols = pl.ds(128 * j, 128)
            up_src = mesh_ref.at[pl.ds(OWN - HALO + 16 * i, 16), cols]
            low_src = mesh_ref.at[pl.ds(16 * i, 16), cols]
            n = i * 4 + j
            halo_copies.append(
                rcopy(up_src, halo.at[0, pl.ds(16 * i, 16), cols], s_halo.at[0, n], r_halo.at[0, n], upper)
            )
            halo_copies.append(
                rcopy(low_src, halo.at[1, pl.ds(16 * i, 16), cols], s_halo.at[1, n], r_halo.at[1, n], lower)
            )
    for cp in halo_copies:
        cp.start()
    for cp in halo_copies:
        cp.wait()
    low = jnp.where(band == 0, 0.0, halo[0].astype(F32)).astype(BF16)
    high = jnp.where(band == 63, 0.0, halo[1].astype(F32)).astype(BF16)
    edge_rows = jnp.concatenate([low, high], axis=0)
    sent_edge = dot(edge_rows, ws_ref[...])
    sent = jnp.concatenate([sent_own, sent_edge], axis=0).astype(BF16)

    agg = jnp.zeros((PTS, D), F32)
    for k in range(3):
        hit = lanes_of((PTS, ROWS)) == index[:, k : k + 1]
        pre = dot(jnp.where(hit, 1.0, 0.0).astype(BF16), sent) + recv_rows
        sig = 0.5 * jnp.tanh(0.5 * pre) + 0.5
        act = pre * sig
        agg = agg + act
        slope_k[k] = sig + act * (1.0 - sig)
    agg_in = agg.astype(BF16)
    hidden = grid_ref[...].astype(F32) + dot(agg_in, we_ref[...])
    inv_rms = lax.rsqrt(jnp.mean(hidden * hidden, axis=1, keepdims=True) + 1e-05)
    gain = gain_ref[...]
    normed = (hidden * inv_rms * gain).astype(BF16)
    pred = dot(normed, wo[...])
    fields[0, 0] = pack_field(pred).astype(BF16)

    def rows(n):
        return pl.ds(64 * n, 64)

    fz = [
        rcopy(fields.at[0, 0, rows(n)], fields.at[1, 0, rows(n)], s_fz.at[n], r_fz.at[n], z_peer(8))
        for n in range(4)
    ]
    fy = [
        rcopy(fields.at[0, 0], fields.at[0, k], s_fy.at[k - 1], r_fy.at[k - 1], y_peer(k))
        for k in (1, 2, 3)
    ]
    fzy = [
        [
            rcopy(
                fields.at[1, 0, rows(n)], fields.at[1, k, rows(n)], s_fzy.at[k - 1, n], r_fzy.at[k - 1, n], y_peer(k)
            )
            for k in (1, 2, 3)
        ]
        for n in range(4)
    ]
    for cp in fz + fy:
        cp.start()

    own = fields[0, 0].astype(F32)
    error = own - truth
    error_sq = error * error + SMOOTH_SQ
    error_inv = lax.rsqrt(error_sq)
    pair_slope = jnp.zeros((PACK, 128), F32)
    spread = jnp.full((PACK, 128), 0.25, F32)

    def pair(h, k, pair_slope, spread):
        differ = own - fields[h, k].astype(F32)
        sq = differ * differ + SMOOTH_SQ
        inv = lax.rsqrt(sq)
        return pair_slope + differ * inv, spread + sq * inv

    for k in (1, 2, 3):
        fy[k - 1].wait_recv()
        pair_slope, spread = pair(0, k, pair_slope, spread)
    for n in range(4):
        fz[n].wait_recv()
        for cp in fzy[n]:
            cp.start()
    pair_slope, spread = pair(1, 0, pair_slope, spread)
    for k in (1, 2, 3):
        for n in range(4):
            fzy[n][k - 1].wait_recv()
        pair_slope, spread = pair(1, k, pair_slope, spread)

    field_grad = (error * error_inv * 0.125 - pair_slope * (1.0 / 56.0)) * (mask * scale)
    grad16 = unpack_field(field_grad).astype(BF16)

    crps = (error_sq * error_inv * 0.125 - spread * (1.0 / 112.0)) * mask
    crps_hi = crps.astype(BF16)
    crps_lo = (crps - crps_hi.astype(F32)).astype(BF16)
    lane8 = lanes_of((8, 128))
    take_main = jnp.where(lane8 < VARS, 1.0, 0.0).astype(BF16)
    take_tail = jnp.where((lane8 >= VARS) & (lane8 < VARS + FOLD), 1.0, 0.0).astype(BF16)
    across = ((1,), (1,))
    main = dot(take_main, crps_hi, across) + dot(take_main, crps_lo, across)
    tail = dot(take_tail, crps_hi, across) + dot(take_tail, crps_lo, across)
    tail = tail[:, :128] + tail[:, 128:]
    tail = tail + pltpu.roll(tail, 64, 1)
    crow[0, :, :256] = main
    crow[0, :, 256:] = tail
    cy = [rcopy(crow.at[0], crow.at[k], s_cy.at[k - 1], r_cy.at[k - 1], y_peer(k)) for k in (1, 2, 3)]
    for cp in cy:
        cp.start()

    def store_part(q, full):
        if q == 3:
            wide = full.reshape(64, 8, 128)
            block = jnp.concatenate([wide, jnp.zeros_like(wide)], axis=1).astype(BF16)
            block = block.reshape(4, 8, 2, 16, 128)
            for cc in range(2):
                part[cc, q, :, :, :, :128] = block[:, :, cc]
                part[cc, q, :, :, :, 128:] = jnp.zeros((4, 8, 16, 128), BF16)
        else:
            left = full[:, :256].reshape(64, 8, 256)
            right = full[:, 256:].reshape(64, 8, 256)
            block = jnp.concatenate([left, right], axis=1).astype(BF16).reshape(4, 8, 2, 16, 256)
            for cc in range(2):
                part[cc, q] = block[:, :, cc]

    core = [rcopy(part.at[1 - c, q], core_in.at[q], s_core.at[q], r_core.at[q], sibling) for q in range(4)]
    depth = ((0,), (0,))
    d_normed = dot(grad16, wo[...], ((1,), (1,)))
    store_part(3, dot(normed, grad16, depth))
    core[3].start()
    gained = d_normed * gain
    mean = jnp.mean(gained * hidden, axis=1, keepdims=True)
    d_hidden = (inv_rms * gained - hidden * (inv_rms * inv_rms * inv_rms * mean)).astype(BF16)
    d_agg = dot(d_hidden, we_ref[...], ((1,), (1,)))
    store_part(2, dot(agg_in, d_hidden, depth))
    core[2].start()
    d_recv = jnp.zeros((PTS, D), F32)
    d_sent = jnp.zeros((ROWS, D), F32)
    for k in range(3):
        d_pre = d_agg * slope_k[k]
        d_recv = d_recv + d_pre
        d_sent = d_sent + dot(onehot_t[k], d_pre.astype(BF16))
    store_part(1, dot(grid_ref[...], d_recv.astype(BF16), depth))
    core[1].start()
    d_sent = d_sent.astype(BF16)
    store_part(0, dot(mesh_ref[...], d_sent[:OWN], depth) + dot(edge_rows, d_sent[OWN:], depth))
    core[0].start()

    x1 = [
        [
            rcopy(
                summed.at[q, (x + k) % 4, pl.ds(0, 4)], x_in1.at[q, k - 1], s_x1.at[q, k - 1], r_x1.at[q, k - 1], x_peer(k)
            )
            for k in (1, 2, 3)
        ]
        for q in range(4)
    ]
    for q in (3, 2, 1, 0):
        core[q].wait_recv()
        summed[q] = (part[c, q].astype(F32) + core_in[q].astype(F32)).astype(BF16)
        for cp in x1[q]:
            cp.start()
    y2 = [
        rcopy(summed.at[(y + k) % 4, :, pl.ds(4, 4)], y_in2.at[k - 1], s_y2.at[k - 1], r_y2.at[k - 1], y_peer(k))
        for k in (1, 2, 3)
    ]
    for cp in y2:
        cp.start()

    for cp in cy:
        cp.wait_recv()
    crow_z[0] = (crow[0] + crow[1]) + (crow[2] + crow[3])
    cz = rcopy(crow_z.at[0], crow_z.at[1], s_cz.at[0], r_cz.at[0], z_peer(8))
    cz.start()

    def add4(a, b0, b1, b2):
        return ((a.astype(F32) + b0.astype(F32)) + (b1.astype(F32) + b2.astype(F32))).astype(BF16)

    y1 = [
        rcopy(x_sum1.at[(y + k) % 4], y_in1.at[k - 1], s_y1.at[k - 1], r_y1.at[k - 1], y_peer(k))
        for k in (1, 2, 3)
    ]
    x2 = [
        rcopy(y_sum2.at[(x + k) % 4], x_in2.at[k - 1], s_x2.at[k - 1], r_x2.at[k - 1], x_peer(k))
        for k in (1, 2, 3)
    ]
    for q in (3, 2, 1, 0):
        for cp in x1[q]:
            cp.wait_recv()
        x_sum1[q] = add4(summed[q, x, 0:4], x_in1[q, 0], x_in1[q, 1], x_in1[q, 2])
    for cp in y1:
        cp.start()
    for cp in y2:
        cp.wait_recv()
    y_sum2[...] = add4(summed[y, :, 4:8], y_in2[0], y_in2[1], y_in2[2])
    for cp in x2:
        cp.start()
    for cp in y1:
        cp.wait_recv()
    slab[0:4] = add4(x_sum1[y], y_in1[0], y_in1[1], y_in1[2])
    for cp in x2:
        cp.wait_recv()
    slab[4:8] = add4(y_sum2[x], x_in2[0], x_in2[1], x_in2[2])

    zs = [
        rcopy(slab.at[(zl + k) % 8], z_in.at[k - 1], s_z.at[k - 1], r_z.at[k - 1], z_peer(k))
        for k in range(1, 16)
    ]
    order = (8, 7, 9, 6, 10, 5, 11, 4, 12, 3, 13, 2, 14, 1, 15)
    for k in order:
        zs[k - 1].start()
    acc = slab[zl].astype(F32)
    for k in reversed(order):
        zs[k - 1].wait_recv()
        acc = acc + z_in[k - 1].astype(F32)
    final[0] = acc
    gy = [rcopy(final.at[0], final.at[k], s_g.at[k - 1], r_g.at[k - 1], y_peer(k)) for k in (1, 2, 3)]
    for cp in gy:
        cp.start()
    cz.wait_recv()
    crps_out[...] = (crow_z[0] + crow_z[1])[:1, :PTS]
    for cp in gy:
        cp.wait_recv()

    def piece(q):
        return final[(y - q + 4) % 4]

    for q, out in ((0, gs_out), (1, gr_out), (2, ge_out)):
        got = piece(q)
        out[:, :256] = got[:8]
        out[:, 256:] = got[8:]
    go_out[...] = piece(3)[:8, :VARS]

    sends = fz + fy + [cp for g in fzy for cp in g] + cy + [cz] + core
    sends += [cp for g in x1 for cp in g] + y1 + y2 + x2 + zs + gy
    for cp in sends:
        cp.wait_send()


def per_device(mesh_latent, grid_latent, senders, live_points, target, w_send, w_recv, w_edge, w_out, gain):
    vmem = pl.BlockSpec(memory_space=pltpu.VMEM)
    dma = pltpu.SemaphoreType.DMA
    shape = jax.ShapeDtypeStruct
    outs = pl.pallas_call(
        kernel,
        out_shape=(
            shape((1, PTS), F32),
            shape((8, D), F32),
            shape((8, D), F32),
            shape((8, D), F32),
            shape((8, VARS), F32),
        ),
        in_specs=[vmem] * 10,
        out_specs=[vmem] * 5,
        scratch_shapes=[
            pltpu.VMEM((2, HALO, D), BF16),
            pltpu.VMEM((D, 128), BF16),
            pltpu.VMEM((128, 384), F32),
            pltpu.VMEM((384, 128), F32),
            pltpu.VMEM((3, ROWS, PTS), BF16),
            pltpu.VMEM((3, PTS, D), F32),
            pltpu.VMEM((2, 4, PACK, 128), BF16),
            pltpu.VMEM((4, 8, 384), F32),
            pltpu.VMEM((2, 8, 384), F32),
            pltpu.VMEM((2, 4, 4, 8, 16, 256), BF16),
            pltpu.VMEM((4, 4, 8, 16, 256), BF16),
            pltpu.VMEM((4, 4, 8, 16, 256), BF16),
            pltpu.VMEM((4, 3, 4, 16, 256), BF16),
            pltpu.VMEM((4, 4, 16, 256), BF16),
            pltpu.VMEM((3, 4, 16, 256), BF16),
            pltpu.VMEM((3, 4, 4, 16, 256), BF16),
            pltpu.VMEM((4, 4, 16, 256), BF16),
            pltpu.VMEM((3, 4, 16, 256), BF16),
            pltpu.VMEM((8, 16, 256), BF16),
            pltpu.VMEM((15, 16, 256), BF16),
            pltpu.VMEM((4, 16, 256), F32),
            dma((2, 8)), dma((2, 8)),
            dma((4,)), dma((4,)),
            dma((3,)), dma((3,)),
            dma((3, 4)), dma((3, 4)),
            dma((3,)), dma((3,)),
            dma((1,)), dma((1,)),
            dma((4,)), dma((4,)),
            dma((4, 3)), dma((4, 3)),
            dma((3,)), dma((3,)),
            dma((3,)), dma((3,)),
            dma((3,)), dma((3,)),
            dma((15,)), dma((15,)),
            dma((3,)), dma((3,)),
        ],
        compiler_params=pltpu.CompilerParams(
            collective_id=0, has_side_effects=True, vmem_limit_bytes=50 * 2**20
        ),
        name="decoder_crps_step",
    )(
        mesh_latent[0], grid_latent[0], senders, live_points.reshape(1, -1), target,
        w_send, w_recv, w_edge, w_out, gain.reshape(1, -1),
    )
    return (outs[0].reshape(PTS), outs[1], outs[2], outs[3], outs[4])


def solution(mesh):
    placed = (
        P("member", "band", None),
        P("member", "band", None),
        P("band", None),
        P(),
        P(None, "band"),
        P(),
        P(),
        P(),
        P(),
        P(),
    )
    return jax.shard_map(
        per_device,
        mesh=mesh,
        in_specs=placed,
        out_specs=(P("band"), P("band", None), P("band", None), P("band", None), P("band", None)),
        check_vma=False,
    )
```

```python
import jax
import jax.numpy as jnp
from jax import lax
from jax.experimental import pallas as pl
from jax.experimental.pallas import tpu as pltpu
from jax.sharding import PartitionSpec as P

HALO = 32
SMOOTH_SQ = 0.0625
MESH = pl.DeviceIdType.MESH
F32 = jnp.float32
BF16 = jnp.bfloat16

D = 512
NCH = 4
PIECE_AT, PIECES = (0, 3, 5), (3, 2, 2)
SLOT_AT, SLOTS = (0, 2, 3), (2, 1, 1)
ORDER_Z = (8, 7, 9, 6, 10, 5, 11, 4, 12, 3, 13, 2, 14, 1, 15)
VMEM_LIMIT = 64 * 2**20 - 2**18
VARS = 100
PTS = 320
OWN = 128
ROWS = OWN + 2 * HALO
PACK = 256
TAIL = PTS - PACK
FOLD = 25


def dot(a, b, dims=((1,), (0,))):
    return lax.dot_general(a, b, (dims, ((), ())), preferred_element_type=F32)


def lanes_of(shape):
    return lax.broadcasted_iota(jnp.int32, shape, 1)


def rows_of(shape):
    return lax.broadcasted_iota(jnp.int32, shape, 0)


def pack_field(x):
    tail = x[PACK:]
    lane = lanes_of(tail.shape)
    inside = (lane >= VARS) & (lane < VARS + FOLD)
    parts = [jnp.where(inside, pltpu.roll(tail, VARS - FOLD * j, 1), 0.0) for j in range(4)]
    return x[:PACK] + jnp.concatenate(parts, axis=0)


def unpack_field(x):
    lane = lanes_of((TAIL, 128))
    tail = jnp.zeros((TAIL, 128), F32)
    for j in range(4):
        moved = pltpu.roll(x[TAIL * j : TAIL * (j + 1)], 128 - (VARS - FOLD * j), 1)
        tail = tail + jnp.where((lane >= FOLD * j) & (lane < FOLD * (j + 1)), moved, 0.0)
    main = jnp.where(lanes_of((PACK, 128)) < VARS, x, 0.0)
    return jnp.concatenate([main, tail], axis=0)


def kernel(
    mesh_hbm, grid_hbm, send_hbm, live_hbm, target_hbm, ws_hbm, wr_hbm, we_hbm, wo_hbm, gain_hbm,
    crow_z, final,
    mesh_ref, grid_ref, send_ref, live_ref, target_ref, ws_ref, wr_ref, we_ref, wo_ref, gain_ref,
    s_in, halo, wo, wpad, tpad, spad, onehot_t, slope_k, fields, crow,
    normed_t, agg_t, grid_t, mesh_t,
    part, part3, core_in, core_in3, summed, summed3, x_in1, x_in3, x_sum1, y_in1, y_in2, y_sum2, x_in2, slab, z_in,
    s_halo, r_halo, s_fz, r_fz, s_fy, r_fy, s_fzy, r_fzy, s_cy, r_cy, s_cz, r_cz,
    ok_far, s_core, r_core, s_x1, r_x1, s_y1, r_y1, s_y2, r_y2, s_x2, r_x2, s_z, r_z, s_g, r_g,
):
    member = lax.axis_index("member")
    band = lax.axis_index("band")
    zh, y = member // 4, member % 4
    x, zl, c = band // 16, (band // 2) % 8, band % 2
    z = zh * 8 + zl

    def dev(z_, y_, x_, c_):
        return ((z_ // 8) * 4 + y_, x_ * 16 + (z_ % 8) * 2 + c_)

    def z_peer(k):
        return dev((z + k) % 16, y, x, c)

    def y_peer(k):
        return dev(z, (y + k) % 4, x, c)

    def x_peer(k):
        return dev(z, y, (x + k) % 4, c)

    sibling = dev(z, y, x, 1 - c)
    other = (member, (band + 2 * c - 1 + 64) % 64)
    far = zl == 7 * c

    def rcopy(src, dst, ss, rs, to):
        return pltpu.make_async_remote_copy(
            src_ref=src, dst_ref=dst, send_sem=ss, recv_sem=rs, device_id=to, device_id_type=MESH
        )

    barrier = pltpu.get_barrier_semaphore()
    peers = [other] + [z_peer(k) for k in ORDER_Z]
    peers += [y_peer(k) for k in (1, 2, 3)] + [x_peer(k) for k in (1, 2, 3)] + [sibling]

    def across(k):
        return dev((z + 8) % 16, (y + k) % 4, x, c)

    def greet(p):
        pl.semaphore_signal(barrier, inc=1, device_id=p, device_id_type=MESH)

    for p in peers:
        greet(p)

    hbm = (mesh_hbm, ws_hbm, grid_hbm, wr_hbm, send_hbm, target_hbm, live_hbm, gain_hbm, wo_hbm, we_hbm)
    near = (mesh_ref, ws_ref, grid_ref, wr_ref, send_ref, target_ref, live_ref, gain_ref, wo_ref, we_ref)
    loads = [pltpu.make_async_copy(a, b, s_in.at[i]) for i, (a, b) in enumerate(zip(hbm, near))]
    for cp in loads:
        cp.start()

    sends, pending = [], {}

    def start(*copies):
        for cp in copies:
            cp.start()
            sends.append(cp)
            pending[id(cp)] = cp

    def arrive(*copies):
        for cp in copies:
            cp.wait_recv()
            del pending[id(cp)]

    def finish():
        arrive(*list(pending.values()))
        for cp in sends:
            cp.wait_send()

    loads[0].wait()
    loads[1].wait()
    sent_own = dot(mesh_ref[...], ws_ref[...])
    loads[2].wait()
    loads[3].wait()
    recv_rows = dot(grid_ref[...], wr_ref[...])
    for cp in loads[4:]:
        cp.wait()
    wpad[...] = jnp.zeros(wpad.shape, F32)
    wpad[:VARS] = wo_ref[...].astype(F32)
    wo[...] = wpad[...].astype(BF16)
    tpad[...] = jnp.zeros(tpad.shape, F32)
    tpad[:VARS, :PTS] = target_ref[...].astype(F32)
    truth = pack_field(jnp.transpose(tpad[...])[:PTS])
    spad[...] = jnp.zeros(spad.shape, F32)
    spad[:3, :PTS] = send_ref[...].astype(F32)
    senders = jnp.transpose(spad[...])[:PTS].astype(jnp.int32)

    low_at = jnp.where(c == 0, OWN, OWN + HALO)
    high_at = jnp.where(c == 0, OWN + HALO, OWN)

    def moved(s):
        return jnp.where(s < HALO, s + low_at, jnp.where(s < HALO + OWN, s - HALO, s - (HALO + OWN) + high_at))

    index = moved(senders)
    index_t = moved(send_ref[...])
    for k in range(3):
        hit = rows_of((ROWS, PTS)) == index_t[k : k + 1, :]
        onehot_t[k] = jnp.where(hit, 1.0, 0.0).astype(BF16)
    live = live_ref[...]
    lane64 = lanes_of(live.shape)
    count = jnp.sum(jnp.where(lane64 == band, live, 0).astype(F32), axis=1, keepdims=True)
    total = jnp.sum(live.astype(F32), axis=1, keepdims=True)
    scale = 1.0 / (total * VARS)
    row = rows_of((PACK, 128))
    lane = lanes_of((PACK, 128))
    point = jnp.where(lane < VARS, row, PACK + row % TAIL)
    mask = jnp.where((lane < VARS + FOLD) & (point.astype(F32) < count), 1.0, 0.0)

    pl.semaphore_wait(barrier, len(peers))

    @pl.when(far)
    def _():
        pl.semaphore_signal(ok_far, inc=1, device_id=z_peer(8), device_id_type=MESH)


    facing = pl.multiple_of((OWN - HALO) * c, HALO)
    behind = pl.multiple_of((OWN - HALO) * (1 - c), HALO)
    halo_copies = []
    for i in range(2):
        for j in range(4):
            n = i * 4 + j
            cols = pl.ds(128 * j, 128)
            src = mesh_ref.at[pl.ds(pl.multiple_of(facing + 16 * i, 16), 16), cols]
            halo_copies.append(rcopy(src, halo.at[0, pl.ds(16 * i, 16), cols], s_halo.at[n], r_halo.at[n], other))
    halo_copies.append(rcopy(mesh_ref.at[pl.ds(behind, HALO)], halo.at[1], s_halo.at[8], r_halo.at[8], sibling))
    start(*halo_copies)
    arrive(*halo_copies)
    polar = (band == 0) | (band == 63)
    outer = jnp.where(polar, 0.0, halo[0].astype(F32)).astype(BF16)
    edge_rows = jnp.concatenate([outer, halo[1]], axis=0)
    sent_edge = dot(edge_rows, ws_ref[...])
    sent = jnp.concatenate([sent_own, sent_edge], axis=0).astype(BF16)

    agg = jnp.zeros((PTS, D), F32)
    for k in range(3):
        hit = lanes_of((PTS, ROWS)) == index[:, k : k + 1]
        pre = dot(jnp.where(hit, 1.0, 0.0).astype(BF16), sent) + recv_rows
        sig = 0.5 * jnp.tanh(0.5 * pre) + 0.5
        act = pre * sig
        agg = agg + act
        slope_k[k] = sig + act * (1.0 - sig)
    agg_in = agg.astype(BF16)
    hidden = grid_ref[...].astype(F32) + dot(agg_in, we_ref[...])
    inv_rms = lax.rsqrt(jnp.mean(hidden * hidden, axis=1, keepdims=True) + 1e-05)
    gain = gain_ref[...]
    normed = (hidden * inv_rms * gain).astype(BF16)
    pred = dot(normed, wo[...], ((1,), (1,)))
    fields[0, 0] = pack_field(pred).astype(BF16)

    def rows(n):
        return pl.ds(PACK // NCH * n, PACK // NCH)

    fz = [
        rcopy(fields.at[0, 0, rows(n)], fields.at[1, 0, rows(n)], s_fz.at[n], r_fz.at[n], z_peer(8))
        for n in range(NCH)
    ]
    fy = [
        rcopy(fields.at[0, 0], fields.at[0, k], s_fy.at[k - 1], r_fy.at[k - 1], y_peer(k))
        for k in (1, 2, 3)
    ]
    fzy = [
        [
            rcopy(
                fields.at[1, 0, rows(n)], fields.at[1, k, rows(n)], s_fzy.at[k - 1, n], r_fzy.at[k - 1, n], y_peer(k)
            )
            for k in (1, 2, 3)
        ]
        for n in range(NCH)
    ]
    straight = [
        rcopy(fields.at[0, 0, rows(n)], fields.at[1, k, rows(n)], s_fzy.at[k - 1, n], r_fzy.at[k - 1, n], across(k))
        for n in range(NCH)
        for k in (1, 2, 3)
    ]
    start(*fz)

    @pl.when(far)
    def _():
        pl.semaphore_wait(ok_far, 1)
        for cp in straight:
            cp.start()

    start(*fy)
    normed_t[...] = jnp.transpose(normed)
    agg_t[...] = jnp.transpose(agg_in)
    grid_t[...] = jnp.transpose(grid_ref[...])
    mesh_t[:, :OWN] = jnp.transpose(mesh_ref[...])
    mesh_t[:, OWN:] = jnp.transpose(edge_rows)

    own = fields[0, 0].astype(F32)
    error = own - truth
    error_sq = error * error + SMOOTH_SQ
    error_inv = lax.rsqrt(error_sq)
    pair_slope = jnp.zeros((PACK, 128), F32)
    spread = jnp.full((PACK, 128), 0.25, F32)

    def pair(h, k, pair_slope, spread):
        differ = own - fields[h, k].astype(F32)
        sq = differ * differ + SMOOTH_SQ
        inv = lax.rsqrt(sq)
        return pair_slope + differ * inv, spread + sq * inv

    for k in (1, 2, 3):
        arrive(fy[k - 1])
        pair_slope, spread = pair(0, k, pair_slope, spread)
    for n in range(NCH):
        arrive(fz[n])

        @pl.when(jnp.logical_not(far))
        def _(n=n):
            for cp in fzy[n]:
                cp.start()

        for cp in fzy[n]:
            sends.append(cp)
            pending[id(cp)] = cp
    pair_slope, spread = pair(1, 0, pair_slope, spread)
    for k in (1, 2, 3):
        for n in range(NCH):
            arrive(fzy[n][k - 1])
        pair_slope, spread = pair(1, k, pair_slope, spread)

    field_grad = (error * error_inv * 0.125 - pair_slope * (1.0 / 56.0)) * (mask * scale)
    grad16 = unpack_field(field_grad).astype(BF16)


    def store_part(q, full):
        for t in range(2):
            halves = [full[:, 256 * t + 128 * i : 256 * t + 128 * (i + 1)].reshape(64, 8, 128) for i in range(2)]
            block = jnp.concatenate(halves, axis=1).astype(BF16).reshape(4, 4, 2, 2, 16, 128)
            for p in range(2):
                for cc in range(2):
                    part[cc, q, t, p] = block[:, :, p, cc]

    def store_head(full):
        bands = full.reshape(4, 4, 2, 2, 8, 128)
        for t in range(2):
            for p in range(2):
                for cc in range(2):
                    two = jnp.concatenate([bands[:, 2 * t, p, cc], bands[:, 2 * t + 1, p, cc]], axis=1)
                    part3[cc, p, t] = two.astype(BF16)

    core = [rcopy(part.at[1 - c, q], core_in.at[q], s_core.at[q], r_core.at[q], sibling) for q in range(3)]
    core.append(rcopy(part3.at[1 - c], core_in3, s_core.at[3], r_core.at[3], sibling))
    d_normed = dot(grad16, wo[...])
    store_head(dot(normed_t[...], grad16))
    start(core[3])
    gained = d_normed * gain
    mean = jnp.mean(gained * hidden, axis=1, keepdims=True)
    d_hidden = (inv_rms * gained - hidden * (inv_rms * inv_rms * inv_rms * mean)).astype(BF16)
    d_agg = dot(d_hidden, we_ref[...], ((1,), (1,)))
    store_part(2, dot(agg_t[...], d_hidden))
    start(core[2])
    d_recv = jnp.zeros((PTS, D), F32)
    d_sent = jnp.zeros((ROWS, D), F32)
    for k in range(3):
        d_pre = d_agg * slope_k[k]
        d_recv = d_recv + d_pre
        d_sent = d_sent + dot(onehot_t[k], d_pre.astype(BF16))
    store_part(1, dot(grid_t[...], d_recv.astype(BF16)))
    start(core[1])
    store_part(0, dot(mesh_t[...], d_sent.astype(BF16)))
    start(core[0])

    crps = (error_sq * error_inv * 0.125 - spread * (1.0 / 112.0)) * mask
    crps_hi = crps.astype(BF16)
    crps_lo = (crps - crps_hi.astype(F32)).astype(BF16)
    lane8 = lanes_of((8, 128))
    take_main = jnp.where(lane8 < VARS, 1.0, 0.0).astype(BF16)
    take_tail = jnp.where((lane8 >= VARS) & (lane8 < VARS + FOLD), 1.0, 0.0).astype(BF16)
    wide = ((1,), (1,))
    main = dot(take_main, crps_hi, wide) + dot(take_main, crps_lo, wide)
    tail = dot(take_tail, crps_hi, wide) + dot(take_tail, crps_lo, wide)
    tail = tail[:, :128] + tail[:, 128:]
    tail = tail + pltpu.roll(tail, 64, 1)
    crow[0, :, :256] = main
    crow[0, :, 256:] = tail
    cy = [rcopy(crow.at[0], crow.at[k], s_cy.at[k - 1], r_cy.at[k - 1], y_peer(k)) for k in (1, 2, 3)]
    start(*cy)

    def x1_copy(k, q):
        to = (x + k) % 4
        src = summed3.at[:, :, to] if q == 3 else summed.at[q, :, :, to, pl.ds(0, 2)]
        dst = x_in3.at[k - 1] if q == 3 else x_in1.at[q, k - 1]
        return rcopy(src, dst, s_x1.at[q, k - 1], r_x1.at[q, k - 1], x_peer(k))

    def y2_copy(k, q):
        to = (y + k) % 4
        src = summed.at[q, to % 2, to // 2, :, pl.ds(2, 2)]
        return rcopy(src, y_in2.at[q, k - 1], s_y2.at[q, k - 1], r_y2.at[q, k - 1], y_peer(k))

    x1 = [[x1_copy(k, q) for k in (1, 2, 3)] for q in range(4)]
    y2 = [[y2_copy(k, q) for k in (1, 2, 3)] for q in range(3)]

    def add(a, b):
        return (a.astype(F32) + b.astype(F32)).astype(BF16)

    for q in (3, 2, 1, 0):
        arrive(core[q])
        if q == 3:
            summed3[...] = add(part3[c], core_in3[...])
            start(*x1[q])
        else:
            summed[q] = add(part[c, q], core_in[q])
            for k in (1, 0, 2):
                start(x1[q][k], y2[q][k])

    arrive(*cy)
    crow_z[0] = (crow[0] + crow[1]) + (crow[2] + crow[3])
    cz = rcopy(crow_z.at[0], crow_z.at[1], s_cz.at[0], r_cz.at[0], z_peer(8))
    start(cz)

    def add4(a, b0, b1, b2):
        return ((a.astype(F32) + b0.astype(F32)) + (b1.astype(F32) + b2.astype(F32))).astype(BF16)

    def y1_copy(k, g):
        n = pl.ds(PIECE_AT[g], PIECES[g])
        return rcopy(x_sum1.at[(y + k) % 4, n], y_in1.at[k - 1, n], s_y1.at[g, k - 1], r_y1.at[g, k - 1], y_peer(k))

    def x2_copy(k, q):
        return rcopy(y_sum2.at[(x + k) % 4, q], x_in2.at[q, k - 1], s_x2.at[q, k - 1], r_x2.at[q, k - 1], x_peer(k))

    y1 = [[y1_copy(k, g) for k in (1, 2, 3)] for g in range(3)]
    x2 = [[x2_copy(k, q) for k in (1, 2, 3)] for q in range(3)]
    for q in (3, 2, 1, 0):
        arrive(*x1[q])
        if q == 3:
            head = add4(summed3[:, :, x], x_in3[0], x_in3[1], x_in3[2])
            for p in range(2):
                for t in range(2):
                    x_sum1[2 * p + t, 0] = head[p, t]
            continue
        g = 2 - q
        at = PIECE_AT[g] + PIECES[g] - 2
        body = add4(summed[q, :, :, x, 0:2], x_in1[q, 0], x_in1[q, 1], x_in1[q, 2])
        for p in range(2):
            for t in range(2):
                x_sum1[2 * p + t, at : at + 2] = body[t, p]
        start(y1[g][1], y1[g][0], y1[g][2])
        arrive(*y2[q])
        y_sum2[:, q] = add4(summed[q, y % 2, y // 2, :, 2:4], y_in2[q, 0], y_in2[q, 1], y_in2[q, 2])
        start(x2[q][1], x2[q][0], x2[q][2])

    away = (zl + y // 2) % 2
    owner = away == 0

    def z_copy(j, g):
        k = 2 * j + away
        n = pl.ds(SLOT_AT[g], SLOTS[g])
        return rcopy(slab.at[((z + k) % 8) // 2, n], z_in.at[k, n], s_z.at[g, j], r_z.at[g, k], z_peer(k))

    def z_arrived(k, g):
        n = pl.ds(SLOT_AT[g], SLOTS[g])
        rcopy(slab.at[0, n], z_in.at[k, n], s_z.at[g, 0], r_z.at[g, k], z_peer(8)).wait_recv()

    def g_copy(k, g):
        n = pl.ds(SLOT_AT[g], SLOTS[g])
        return rcopy(final.at[y % 2, n], final.at[y % 2, n], s_g.at[g, k - 1], r_g.at[g, y % 2], y_peer(k))

    for g in range(3):
        q = 2 - g
        lo, hi = SLOT_AT[g], SLOT_AT[g] + SLOTS[g]
        arrive(*y1[g])
        n = pl.ds(PIECE_AT[g], PIECES[g])
        done1 = add4(x_sum1[y, n], y_in1[0, n], y_in1[1, n], y_in1[2, n])
        if g == 0:
            for h in range(4):
                slab[h, 0] = done1[0]
        for h in range(2):
            slab[h, hi - 1] = done1[PIECES[g] - 2 + h]
        arrive(*x2[q])
        done2 = add4(y_sum2[x, q], x_in2[q, 0], x_in2[q, 1], x_in2[q, 2])
        for h in range(2):
            slab[2 + h, hi - 1] = done2[h]
        for j in (4, 3, 5, 2, 6, 1, 7):
            z_copy(j, g).start()

        @pl.when(away == 1)
        def _(g=g):
            z_copy(0, g).start()


    @pl.when(owner)
    def _():
        for g in range(3):
            n = pl.ds(SLOT_AT[g], SLOTS[g])
            acc = slab[zl // 2, n].astype(F32)
            for k in (1, 15, 2, 14, 3, 13, 4, 12, 5, 11, 6, 10, 7, 9, 8):
                z_arrived(k, g)
                acc = acc + z_in[k, n].astype(F32)
            final[y % 2, n] = acc
            for k in (2, 1, 3):
                g_copy(k, g).start()

    arrive(cz)
    for t in range(2):

        @pl.when(jnp.logical_not(owner & (y % 2 == t)))
        def _(t=t):
            for g in range(3):
                n = pl.ds(SLOT_AT[g], SLOTS[g])
                rcopy(final.at[t, n], final.at[t, n], s_g.at[g, 0], r_g.at[g, t], z_peer(8)).wait_recv()

    @pl.when(owner)
    def _():
        for g in range(3):
            for k in (1, 2, 3):
                g_copy(k, g).wait_send()

    @pl.when(away == 1)
    def _():
        for g in range(3):
            z_copy(0, g).wait_send()

    for g in range(3):
        for j in range(1, 8):
            z_copy(j, g).wait_send()
    finish()


def unpack(crow_ref, final_ref, crps_out, gs_out, gr_out, ge_out, go_out):
    zl = (lax.axis_index("band") // 2) % 8
    crps_out[...] = (crow_ref[0] + crow_ref[1])[0, :PTS]
    for q, out in ((0, gs_out), (1, gr_out), (2, ge_out)):
        for t in range(2):
            got = final_ref[t, 3 - q]
            out[:, 256 * t : 256 * t + 128] = got[:8]
            out[:, 256 * t + 128 : 256 * t + 256] = got[8:]
    got = final_ref[zl // 4, 0]
    go_out[...] = jnp.where((zl // 2) % 2 == 0, got[:8, :VARS], got[8:, :VARS])


def per_device(mesh_latent, grid_latent, senders, live_points, target, w_send, w_recv, w_edge, w_out, gain):
    vmem = pl.BlockSpec(memory_space=pltpu.VMEM)
    dma = pltpu.SemaphoreType.DMA
    shape = jax.ShapeDtypeStruct
    args = (
        mesh_latent[0], grid_latent[0], senders.T, live_points.reshape(1, -1), target,
        w_send, w_recv, w_edge, w_out.T, gain.reshape(1, -1),
    )
    crow, final = pl.pallas_call(
        kernel,
        out_shape=(shape((2, 8, 384), F32), shape((2, 4, 16, 128), F32)),
        in_specs=[pl.BlockSpec(memory_space=pltpu.HBM)] * 10,
        out_specs=[vmem] * 2,
        scratch_shapes=[pltpu.VMEM(a.shape, a.dtype) for a in args]
        + [
            dma((10,)),
            pltpu.VMEM((2, HALO, D), BF16),
            pltpu.VMEM((128, D), BF16),
            pltpu.VMEM((128, D), F32),
            pltpu.VMEM((128, 384), F32),
            pltpu.VMEM((128, 384), F32),
            pltpu.VMEM((3, ROWS, PTS), BF16),
            pltpu.VMEM((3, PTS, D), F32),
            pltpu.VMEM((2, 4, PACK, 128), BF16),
            pltpu.VMEM((4, 8, 384), F32),
            pltpu.VMEM((D, PTS), BF16),
            pltpu.VMEM((D, PTS), BF16),
            pltpu.VMEM((D, PTS), BF16),
            pltpu.VMEM((D, ROWS), BF16),
            pltpu.VMEM((2, 3, 2, 2, 4, 4, 16, 128), BF16),
            pltpu.VMEM((2, 2, 2, 4, 16, 128), BF16),
            pltpu.VMEM((3, 2, 2, 4, 4, 16, 128), BF16),
            pltpu.VMEM((2, 2, 4, 16, 128), BF16),
            pltpu.VMEM((3, 2, 2, 4, 4, 16, 128), BF16),
            pltpu.VMEM((2, 2, 4, 16, 128), BF16),
            pltpu.VMEM((3, 3, 2, 2, 2, 16, 128), BF16),
            pltpu.VMEM((3, 2, 2, 16, 128), BF16),
            pltpu.VMEM((4, 7, 16, 128), BF16),
            pltpu.VMEM((3, 7, 16, 128), BF16),
            pltpu.VMEM((3, 3, 4, 2, 16, 128), BF16),
            pltpu.VMEM((4, 3, 2, 16, 128), BF16),
            pltpu.VMEM((3, 3, 2, 16, 128), BF16),
            pltpu.VMEM((4, 4, 16, 128), BF16),
            pltpu.VMEM((16, 4, 16, 128), BF16),
            dma((9,)), dma((9,)),
            dma((NCH,)), dma((NCH,)),
            dma((3,)), dma((3,)),
            dma((3, NCH)), dma((3, NCH)),
            dma((3,)), dma((3,)),
            dma((1,)), dma((1,)),
            pltpu.SemaphoreType.REGULAR,
            dma((4,)), dma((4,)),
            dma((4, 3)), dma((4, 3)),
            dma((3, 3)), dma((3, 3)),
            dma((3, 3)), dma((3, 3)),
            dma((3, 3)), dma((3, 3)),
            dma((3, 8)), dma((3, 16)),
            dma((3, 3)), dma((3, 2)),
        ],
        compiler_params=pltpu.CompilerParams(
            collective_id=0, has_side_effects=True, vmem_limit_bytes=VMEM_LIMIT
        ),
        name="decoder_crps_step",
    )(*args)
    outs = pl.pallas_call(
        unpack,
        out_shape=(
            shape((PTS,), F32),
            shape((8, D), F32),
            shape((8, D), F32),
            shape((8, D), F32),
            shape((8, VARS), F32),
        ),
        in_specs=[vmem] * 2,
        out_specs=[vmem] * 5,
        compiler_params=pltpu.CompilerParams(vmem_limit_bytes=VMEM_LIMIT),
        name="unpack",
    )(crow, final)
    return outs


def solution(mesh):
    placed = (
        P("member", "band", None),
        P("member", "band", None),
        P("band", None),
        P(),
        P(None, "band"),
        P(),
        P(),
        P(),
        P(),
        P(),
    )
    return jax.shard_map(
        per_device,
        mesh=mesh,
        in_specs=placed,
        out_specs=(P("band"), P("band", None), P("band", None), P("band", None), P("band", None)),
        check_vma=False,
    )
```

```python
import jax
import jax.numpy as jnp
from jax import lax
from jax.experimental import pallas as pl
from jax.experimental.pallas import tpu as pltpu
from jax.sharding import PartitionSpec as P

HALO = 32
SMOOTH_SQ = 0.0625
MESH = pl.DeviceIdType.MESH
F32 = jnp.float32
BF16 = jnp.bfloat16

D = 512
NCH = 4
LEG = 3
PIECE_AT, PIECES = (0, 3, 5), (3, 2, 2)
SLOT_AT, SLOTS = (0, 2, 3), (2, 1, 1)
ORDER_Z = (8, 7, 9, 6, 10, 5, 11, 4, 12, 3, 13, 2, 14, 1, 15)
VMEM_LIMIT = 64 * 2**20 - 2**18
VARS = 100
PTS = 320
OWN = 128
ROWS = OWN + 2 * HALO
PACK = 256
TAIL = PTS - PACK
FOLD = 25


def dot(a, b, dims=((1,), (0,))):
    return lax.dot_general(a, b, (dims, ((), ())), preferred_element_type=F32)


def lanes_of(shape):
    return lax.broadcasted_iota(jnp.int32, shape, 1)


def rows_of(shape):
    return lax.broadcasted_iota(jnp.int32, shape, 0)


def pack_field(x):
    tail = x[PACK:]
    lane = lanes_of(tail.shape)
    inside = (lane >= VARS) & (lane < VARS + FOLD)
    parts = [jnp.where(inside, pltpu.roll(tail, VARS - FOLD * j, 1), 0.0) for j in range(4)]
    return x[:PACK] + jnp.concatenate(parts, axis=0)


def unpack_field(x):
    lane = lanes_of((TAIL, 128))
    tail = jnp.zeros((TAIL, 128), F32)
    for j in range(4):
        moved = pltpu.roll(x[TAIL * j : TAIL * (j + 1)], 128 - (VARS - FOLD * j), 1)
        tail = tail + jnp.where((lane >= FOLD * j) & (lane < FOLD * (j + 1)), moved, 0.0)
    main = jnp.where(lanes_of((PACK, 128)) < VARS, x, 0.0)
    return jnp.concatenate([main, tail], axis=0)


def kernel(
    mesh_hbm, grid_hbm, send_hbm, live_hbm, target_hbm, ws_hbm, wr_hbm, we_hbm, wo_hbm, gain_hbm,
    crow_z, final,
    mesh_ref, grid_ref, send_ref, live_ref, target_ref, ws_ref, wr_ref, we_ref, wo_ref, gain_ref,
    s_in, halo, held, wo, wpad, tpad, spad, onehot_t, slope_k, fields, crow,
    normed_t, agg_t, grid_t, mesh_t,
    part, part3, core_in, core_in3, summed, summed3, x_in1, x_in3, x_sum1, y_in1, y_in2, y_sum2, x_in2, slab, z_in,
    s_halo, r_halo, s_fz, r_fz, s_fy, r_fy, s_fzy, r_fzy, s_cy, r_cy, s_cz, r_cz,
    ok_z, ok_far, s_held, r_held, s_core, r_core, s_x1, r_x1, s_y1, r_y1, s_y2, r_y2, s_x2, r_x2, s_z, r_z, s_g, r_g,
):
    member = lax.axis_index("member")
    band = lax.axis_index("band")
    zh, y = member // 4, member % 4
    x, zl, c = band // 16, (band // 2) % 8, band % 2
    z = zh * 8 + zl

    def dev(z_, y_, x_, c_):
        return ((z_ // 8) * 4 + y_, x_ * 16 + (z_ % 8) * 2 + c_)

    def z_peer(k):
        return dev((z + k) % 16, y, x, c)

    def y_peer(k):
        return dev(z, (y + k) % 4, x, c)

    def x_peer(k):
        return dev(z, y, (x + k) % 4, c)

    sibling = dev(z, y, x, 1 - c)
    other = (member, (band + 2 * c - 1 + 64) % 64)
    far = zl == 7 * c
    near = jnp.logical_not(far)
    relay = zl == LEG + (7 - 2 * LEG) * c
    beyond = (member, (band + (2 * LEG + 1) * (2 * c - 1) + 64) % 64)
    to_relay = z_peer(LEG * (1 - 2 * c) + 16)

    def rcopy(src, dst, ss, rs, to):
        return pltpu.make_async_remote_copy(
            src_ref=src, dst_ref=dst, send_sem=ss, recv_sem=rs, device_id=to, device_id_type=MESH
        )

    barrier = pltpu.get_barrier_semaphore()

    def across(k):
        return dev((z + 8) % 16, (y + k) % 4, x, c)

    def greet(p):
        pl.semaphore_signal(barrier, inc=1, device_id=p, device_id_type=MESH)

    @pl.when(far)
    def _():
        greet(beyond)

    @pl.when(near)
    def _():
        greet(other)

    peers = [z_peer(k) for k in (4, 12, 3, 13, 2, 14, 1, 15)]
    peers += [y_peer(k) for k in (2, 1, 3)] + [x_peer(k) for k in (2, 1, 3)] + [sibling]
    for p in peers:
        greet(p)

    hbm = (mesh_hbm, ws_hbm, grid_hbm, wr_hbm, send_hbm, target_hbm, live_hbm, gain_hbm, wo_hbm, we_hbm)
    here = (mesh_ref, ws_ref, grid_ref, wr_ref, send_ref, target_ref, live_ref, gain_ref, wo_ref, we_ref)
    loads = [pltpu.make_async_copy(a, b, s_in.at[i]) for i, (a, b) in enumerate(zip(hbm, here))]
    for cp in loads:
        cp.start()

    sends, pending = [], {}

    def start(*copies):
        for cp in copies:
            cp.start()
            sends.append(cp)
            pending[id(cp)] = cp

    def arrive(*copies):
        for cp in copies:
            cp.wait_recv()
            del pending[id(cp)]

    def finish():
        arrive(*list(pending.values()))
        for cp in sends:
            cp.wait_send()

    loads[0].wait()
    loads[1].wait()
    sent_own = dot(mesh_ref[...], ws_ref[...])
    loads[2].wait()
    loads[3].wait()
    recv_rows = dot(grid_ref[...], wr_ref[...])
    pl.semaphore_wait(barrier, len(peers) + jnp.where(near, 1, 0) + jnp.where(relay, 1, 0))
    for k in (4, 12):
        pl.semaphore_signal(ok_z, inc=1, device_id=z_peer(k), device_id_type=MESH)

    facing = pl.multiple_of((OWN - HALO) * c, HALO)
    behind = pl.multiple_of((OWN - HALO) * (1 - c), HALO)
    tiles = [(i, j) for i in range(2) for j in range(4)]

    def tile(ref, n, base=0):
        i, j = tiles[n]
        return ref.at[pl.ds(pl.multiple_of(base + 16 * i, 16), 16), pl.ds(128 * j, 128)]

    direct, first_leg, second_leg = [], [], []
    for n in range(8):
        mine = tile(mesh_ref, n, facing)
        direct.append(rcopy(mine, tile(halo.at[0], n), s_halo.at[n], r_halo.at[n], other))
        first_leg.append(rcopy(mine, tile(held, n), s_halo.at[n], r_held.at[n], to_relay))
        second_leg.append(rcopy(tile(held, n), tile(halo.at[0], n), s_held.at[n], r_halo.at[n], beyond))

    @pl.when(far)
    def _():
        for cp in first_leg:
            cp.start()

    @pl.when(near)
    def _():
        for cp in direct:
            cp.start()

    close = rcopy(mesh_ref.at[pl.ds(behind, HALO)], halo.at[1], s_halo.at[8], r_halo.at[8], sibling)
    start(close)

    for cp in loads[4:]:
        cp.wait()
    wpad[...] = jnp.zeros(wpad.shape, F32)
    wpad[:VARS] = wo_ref[...].astype(F32)
    wo[...] = wpad[...].astype(BF16)
    tpad[...] = jnp.zeros(tpad.shape, F32)
    tpad[:VARS, :PTS] = target_ref[...].astype(F32)
    truth = pack_field(jnp.transpose(tpad[...])[:PTS])
    spad[...] = jnp.zeros(spad.shape, F32)
    spad[:3, :PTS] = send_ref[...].astype(F32)
    senders = jnp.transpose(spad[...])[:PTS].astype(jnp.int32)

    low_at = jnp.where(c == 0, OWN, OWN + HALO)
    high_at = jnp.where(c == 0, OWN + HALO, OWN)

    def moved(s):
        return jnp.where(s < HALO, s + low_at, jnp.where(s < HALO + OWN, s - HALO, s - (HALO + OWN) + high_at))

    index = moved(senders)
    index_t = moved(send_ref[...])
    for k in range(3):
        hit = rows_of((ROWS, PTS)) == index_t[k : k + 1, :]
        onehot_t[k] = jnp.where(hit, 1.0, 0.0).astype(BF16)
    live = live_ref[...]
    lane64 = lanes_of(live.shape)
    count = jnp.sum(jnp.where(lane64 == band, live, 0).astype(F32), axis=1, keepdims=True)
    total = jnp.sum(live.astype(F32), axis=1, keepdims=True)
    scale = 1.0 / (total * VARS)
    row = rows_of((PACK, 128))
    lane = lanes_of((PACK, 128))
    point = jnp.where(lane < VARS, row, PACK + row % TAIL)
    mask = jnp.where((lane < VARS + FOLD) & (point.astype(F32) < count), 1.0, 0.0)

    @pl.when(far)
    def _():
        pl.semaphore_wait(ok_z, 2)
        for k in (2, 1, 3):
            pl.semaphore_signal(ok_far, inc=1, device_id=y_peer(k), device_id_type=MESH)

    @pl.when(relay)
    def _():
        for n in range(8):
            first_leg[n].wait_recv()
            second_leg[n].start()

    arrive(close)
    for cp in direct:
        cp.wait_recv()
    polar = (band == 0) | (band == 63)
    outer = jnp.where(polar, 0.0, halo[0].astype(F32)).astype(BF16)
    edge_rows = jnp.concatenate([outer, halo[1]], axis=0)
    sent_edge = dot(edge_rows, ws_ref[...])
    sent = jnp.concatenate([sent_own, sent_edge], axis=0).astype(BF16)

    agg = jnp.zeros((PTS, D), F32)
    for k in range(3):
        hit = lanes_of((PTS, ROWS)) == index[:, k : k + 1]
        pre = dot(jnp.where(hit, 1.0, 0.0).astype(BF16), sent) + recv_rows
        sig = 0.5 * jnp.tanh(0.5 * pre) + 0.5
        act = pre * sig
        agg = agg + act
        slope_k[k] = sig + act * (1.0 - sig)
    agg_in = agg.astype(BF16)
    hidden = grid_ref[...].astype(F32) + dot(agg_in, we_ref[...])
    inv_rms = lax.rsqrt(jnp.mean(hidden * hidden, axis=1, keepdims=True) + 1e-05)
    gain = gain_ref[...]
    normed = (hidden * inv_rms * gain).astype(BF16)
    pred = dot(normed, wo[...], ((1,), (1,)))
    fields[0, 0] = pack_field(pred).astype(BF16)

    def rows(n):
        return pl.ds(PACK // NCH * n, PACK // NCH)

    fz = [
        rcopy(fields.at[0, 0, rows(n)], fields.at[1, 0, rows(n)], s_fz.at[n], r_fz.at[n], z_peer(8))
        for n in range(NCH)
    ]
    fy = [
        rcopy(fields.at[0, 0], fields.at[0, k], s_fy.at[k - 1], r_fy.at[k - 1], y_peer(k))
        for k in (1, 2, 3)
    ]
    fzy = [
        [
            rcopy(
                fields.at[1, 0, rows(n)], fields.at[1, k, rows(n)], s_fzy.at[k - 1, n], r_fzy.at[k - 1, n], y_peer(k)
            )
            for k in (1, 2, 3)
        ]
        for n in range(NCH)
    ]
    straight = [
        rcopy(fields.at[0, 0, rows(n)], fields.at[1, k, rows(n)], s_fzy.at[k - 1, n], r_fzy.at[k - 1, n], across(k))
        for n in range(NCH)
        for k in (2,)
    ]

    @pl.when(near)
    def _():
        pl.semaphore_wait(ok_z, 2)

    start(*fz)

    @pl.when(far)
    def _():
        pl.semaphore_wait(ok_far, 3)
        for cp in straight:
            cp.start()

    start(*fy)
    normed_t[...] = jnp.transpose(normed)
    agg_t[...] = jnp.transpose(agg_in)
    grid_t[...] = jnp.transpose(grid_ref[...])
    mesh_t[:, :OWN] = jnp.transpose(mesh_ref[...])
    mesh_t[:, OWN:] = jnp.transpose(edge_rows)

    own = fields[0, 0].astype(F32)
    error = own - truth
    error_sq = error * error + SMOOTH_SQ
    error_inv = lax.rsqrt(error_sq)
    pair_slope = jnp.zeros((PACK, 128), F32)
    spread = jnp.full((PACK, 128), 0.25, F32)

    def pair(h, k, pair_slope, spread):
        differ = own - fields[h, k].astype(F32)
        sq = differ * differ + SMOOTH_SQ
        inv = lax.rsqrt(sq)
        return pair_slope + differ * inv, spread + sq * inv

    for k in (1, 2, 3):
        arrive(fy[k - 1])
        pair_slope, spread = pair(0, k, pair_slope, spread)
    for n in range(NCH):
        arrive(fz[n])

        fzy[n][0].start()
        fzy[n][2].start()

        @pl.when(near)
        def _(n=n):
            fzy[n][1].start()

        for cp in fzy[n]:
            sends.append(cp)
            pending[id(cp)] = cp
    pair_slope, spread = pair(1, 0, pair_slope, spread)
    for k in (1, 2, 3):
        for n in range(NCH):
            arrive(fzy[n][k - 1])
        pair_slope, spread = pair(1, k, pair_slope, spread)

    field_grad = (error * error_inv * 0.125 - pair_slope * (1.0 / 56.0)) * (mask * scale)
    grad16 = unpack_field(field_grad).astype(BF16)


    def store_part(q, full):
        for t in range(2):
            halves = [full[:, 256 * t + 128 * i : 256 * t + 128 * (i + 1)].reshape(64, 8, 128) for i in range(2)]
            block = jnp.concatenate(halves, axis=1).astype(BF16).reshape(4, 4, 2, 2, 16, 128)
            for p in range(2):
                for cc in range(2):
                    part[cc, q, t, p] = block[:, :, p, cc]

    def store_head(full):
        bands = full.reshape(4, 4, 2, 2, 8, 128)
        for t in range(2):
            for p in range(2):
                for cc in range(2):
                    two = jnp.concatenate([bands[:, 2 * t, p, cc], bands[:, 2 * t + 1, p, cc]], axis=1)
                    part3[cc, p, t] = two.astype(BF16)

    core = [rcopy(part.at[1 - c, q], core_in.at[q], s_core.at[q], r_core.at[q], sibling) for q in range(3)]
    core.append(rcopy(part3.at[1 - c], core_in3, s_core.at[3], r_core.at[3], sibling))
    d_normed = dot(grad16, wo[...])
    store_head(dot(normed_t[...], grad16))
    start(core[3])
    gained = d_normed * gain
    mean = jnp.mean(gained * hidden, axis=1, keepdims=True)
    d_hidden = (inv_rms * gained - hidden * (inv_rms * inv_rms * inv_rms * mean)).astype(BF16)
    d_agg = dot(d_hidden, we_ref[...], ((1,), (1,)))
    store_part(2, dot(agg_t[...], d_hidden))
    start(core[2])
    d_recv = jnp.zeros((PTS, D), F32)
    d_sent = jnp.zeros((ROWS, D), F32)
    for k in range(3):
        d_pre = d_agg * slope_k[k]
        d_recv = d_recv + d_pre
        d_sent = d_sent + dot(onehot_t[k], d_pre.astype(BF16))
    store_part(1, dot(grid_t[...], d_recv.astype(BF16)))
    start(core[1])
    store_part(0, dot(mesh_t[...], d_sent.astype(BF16)))
    start(core[0])

    crps = (error_sq * error_inv * 0.125 - spread * (1.0 / 112.0)) * mask
    crps_hi = crps.astype(BF16)
    crps_lo = (crps - crps_hi.astype(F32)).astype(BF16)
    lane8 = lanes_of((8, 128))
    take_main = jnp.where(lane8 < VARS, 1.0, 0.0).astype(BF16)
    take_tail = jnp.where((lane8 >= VARS) & (lane8 < VARS + FOLD), 1.0, 0.0).astype(BF16)
    wide = ((1,), (1,))
    main = dot(take_main, crps_hi, wide) + dot(take_main, crps_lo, wide)
    tail = dot(take_tail, crps_hi, wide) + dot(take_tail, crps_lo, wide)
    tail = tail[:, :128] + tail[:, 128:]
    tail = tail + pltpu.roll(tail, 64, 1)
    crow[0, :, :256] = main
    crow[0, :, 256:] = tail
    cy = [rcopy(crow.at[0], crow.at[k], s_cy.at[k - 1], r_cy.at[k - 1], y_peer(k)) for k in (1, 2, 3)]
    start(*cy)

    def x1_copy(k, q):
        to = (x + k) % 4
        src = summed3.at[:, :, to] if q == 3 else summed.at[q, :, :, to, pl.ds(0, 2)]
        dst = x_in3.at[k - 1] if q == 3 else x_in1.at[q, k - 1]
        return rcopy(src, dst, s_x1.at[q, k - 1], r_x1.at[q, k - 1], x_peer(k))

    def y2_copy(k, q):
        to = (y + k) % 4
        src = summed.at[q, to % 2, to // 2, :, pl.ds(2, 2)]
        return rcopy(src, y_in2.at[q, k - 1], s_y2.at[q, k - 1], r_y2.at[q, k - 1], y_peer(k))

    x1 = [[x1_copy(k, q) for k in (1, 2, 3)] for q in range(4)]
    y2 = [[y2_copy(k, q) for k in (1, 2, 3)] for q in range(3)]

    def add(a, b):
        return (a.astype(F32) + b.astype(F32)).astype(BF16)

    for q in (3, 2, 1, 0):
        arrive(core[q])
        if q == 3:
            summed3[...] = add(part3[c], core_in3[...])
            start(*x1[q])
        else:
            summed[q] = add(part[c, q], core_in[q])
            for k in (1, 0, 2):
                start(x1[q][k], y2[q][k])

    arrive(*cy)
    crow_z[0] = (crow[0] + crow[1]) + (crow[2] + crow[3])
    cz = rcopy(crow_z.at[0], crow_z.at[1], s_cz.at[0], r_cz.at[0], z_peer(8))
    start(cz)

    def add4(a, b0, b1, b2):
        return ((a.astype(F32) + b0.astype(F32)) + (b1.astype(F32) + b2.astype(F32))).astype(BF16)

    def y1_copy(k, g):
        n = pl.ds(PIECE_AT[g], PIECES[g])
        return rcopy(x_sum1.at[(y + k) % 4, n], y_in1.at[k - 1, n], s_y1.at[g, k - 1], r_y1.at[g, k - 1], y_peer(k))

    def x2_copy(k, q):
        return rcopy(y_sum2.at[(x + k) % 4, q], x_in2.at[q, k - 1], s_x2.at[q, k - 1], r_x2.at[q, k - 1], x_peer(k))

    y1 = [[y1_copy(k, g) for k in (1, 2, 3)] for g in range(3)]
    x2 = [[x2_copy(k, q) for k in (1, 2, 3)] for q in range(3)]
    for q in (3, 2, 1, 0):
        arrive(*x1[q])
        if q == 3:
            head = add4(summed3[:, :, x], x_in3[0], x_in3[1], x_in3[2])
            for p in range(2):
                for t in range(2):
                    x_sum1[2 * p + t, 0] = head[p, t]
            continue
        g = 2 - q
        at = PIECE_AT[g] + PIECES[g] - 2
        body = add4(summed[q, :, :, x, 0:2], x_in1[q, 0], x_in1[q, 1], x_in1[q, 2])
        for p in range(2):
            for t in range(2):
                x_sum1[2 * p + t, at : at + 2] = body[t, p]
        start(y1[g][1], y1[g][0], y1[g][2])
        arrive(*y2[q])
        y_sum2[:, q] = add4(summed[q, y % 2, y // 2, :, 2:4], y_in2[q, 0], y_in2[q, 1], y_in2[q, 2])
        start(x2[q][1], x2[q][0], x2[q][2])

    away = (zl + y // 2) % 2
    owner = away == 0

    def z_copy(j, g):
        k = 2 * j + away
        n = pl.ds(SLOT_AT[g], SLOTS[g])
        return rcopy(slab.at[((z + k) % 8) // 2, n], z_in.at[k, n], s_z.at[g, j], r_z.at[g, k], z_peer(k))

    def z_arrived(k, g):
        n = pl.ds(SLOT_AT[g], SLOTS[g])
        rcopy(slab.at[0, n], z_in.at[k, n], s_z.at[g, 0], r_z.at[g, k], z_peer(8)).wait_recv()

    def g_copy(k, g):
        n = pl.ds(SLOT_AT[g], SLOTS[g])
        return rcopy(final.at[y % 2, n], final.at[y % 2, n], s_g.at[g, k - 1], r_g.at[g, y % 2], y_peer(k))

    for g in range(3):
        q = 2 - g
        lo, hi = SLOT_AT[g], SLOT_AT[g] + SLOTS[g]
        arrive(*y1[g])
        n = pl.ds(PIECE_AT[g], PIECES[g])
        done1 = add4(x_sum1[y, n], y_in1[0, n], y_in1[1, n], y_in1[2, n])
        if g == 0:
            for h in range(4):
                slab[h, 0] = done1[0]
        for h in range(2):
            slab[h, hi - 1] = done1[PIECES[g] - 2 + h]
        arrive(*x2[q])
        done2 = add4(y_sum2[x, q], x_in2[q, 0], x_in2[q, 1], x_in2[q, 2])
        for h in range(2):
            slab[2 + h, hi - 1] = done2[h]
        for j in (4, 3, 5, 2, 6, 1, 7):
            z_copy(j, g).start()

        @pl.when(away == 1)
        def _(g=g):
            z_copy(0, g).start()


    @pl.when(owner)
    def _():
        for g in range(3):
            n = pl.ds(SLOT_AT[g], SLOTS[g])
            acc = slab[zl // 2, n].astype(F32)
            for k in (1, 15, 2, 14, 3, 13, 4, 12, 5, 11, 6, 10, 7, 9, 8):
                z_arrived(k, g)
                acc = acc + z_in[k, n].astype(F32)
            final[y % 2, n] = acc
            for k in (2, 1, 3):
                g_copy(k, g).start()

    arrive(cz)
    for t in range(2):

        @pl.when(jnp.logical_not(owner & (y % 2 == t)))
        def _(t=t):
            for g in range(3):
                n = pl.ds(SLOT_AT[g], SLOTS[g])
                rcopy(final.at[t, n], final.at[t, n], s_g.at[g, 0], r_g.at[g, t], z_peer(8)).wait_recv()

    @pl.when(owner)
    def _():
        for g in range(3):
            for k in (1, 2, 3):
                g_copy(k, g).wait_send()

    @pl.when(away == 1)
    def _():
        for g in range(3):
            z_copy(0, g).wait_send()

    for g in range(3):
        for j in range(1, 8):
            z_copy(j, g).wait_send()
    for cp in direct:
        cp.wait_send()

    @pl.when(relay)
    def _():
        for cp in second_leg:
            cp.wait_send()

    finish()


def unpack(crow_ref, final_ref, crps_out, gs_out, gr_out, ge_out, go_out):
    zl = (lax.axis_index("band") // 2) % 8
    crps_out[...] = (crow_ref[0] + crow_ref[1])[0, :PTS]
    for q, out in ((0, gs_out), (1, gr_out), (2, ge_out)):
        for t in range(2):
            got = final_ref[t, 3 - q]
            out[:, 256 * t : 256 * t + 128] = got[:8]
            out[:, 256 * t + 128 : 256 * t + 256] = got[8:]
    got = final_ref[zl // 4, 0]
    go_out[...] = jnp.where((zl // 2) % 2 == 0, got[:8, :VARS], got[8:, :VARS])


def per_device(mesh_latent, grid_latent, senders, live_points, target, w_send, w_recv, w_edge, w_out, gain):
    vmem = pl.BlockSpec(memory_space=pltpu.VMEM)
    dma = pltpu.SemaphoreType.DMA
    shape = jax.ShapeDtypeStruct
    args = (
        mesh_latent[0], grid_latent[0], senders.T, live_points.reshape(1, -1), target,
        w_send, w_recv, w_edge, w_out.T, gain.reshape(1, -1),
    )
    crow, final = pl.pallas_call(
        kernel,
        out_shape=(shape((2, 8, 384), F32), shape((2, 4, 16, 128), F32)),
        in_specs=[pl.BlockSpec(memory_space=pltpu.HBM)] * 10,
        out_specs=[vmem] * 2,
        scratch_shapes=[pltpu.VMEM(a.shape, a.dtype) for a in args]
        + [
            dma((10,)),
            pltpu.VMEM((2, HALO, D), BF16),
            pltpu.VMEM((HALO, D), BF16),
            pltpu.VMEM((128, D), BF16),
            pltpu.VMEM((128, D), F32),
            pltpu.VMEM((128, 384), F32),
            pltpu.VMEM((128, 384), F32),
            pltpu.VMEM((3, ROWS, PTS), BF16),
            pltpu.VMEM((3, PTS, D), F32),
            pltpu.VMEM((2, 4, PACK, 128), BF16),
            pltpu.VMEM((4, 8, 384), F32),
            pltpu.VMEM((D, PTS), BF16),
            pltpu.VMEM((D, PTS), BF16),
            pltpu.VMEM((D, PTS), BF16),
            pltpu.VMEM((D, ROWS), BF16),
            pltpu.VMEM((2, 3, 2, 2, 4, 4, 16, 128), BF16),
            pltpu.VMEM((2, 2, 2, 4, 16, 128), BF16),
            pltpu.VMEM((3, 2, 2, 4, 4, 16, 128), BF16),
            pltpu.VMEM((2, 2, 4, 16, 128), BF16),
            pltpu.VMEM((3, 2, 2, 4, 4, 16, 128), BF16),
            pltpu.VMEM((2, 2, 4, 16, 128), BF16),
            pltpu.VMEM((3, 3, 2, 2, 2, 16, 128), BF16),
            pltpu.VMEM((3, 2, 2, 16, 128), BF16),
            pltpu.VMEM((4, 7, 16, 128), BF16),
            pltpu.VMEM((3, 7, 16, 128), BF16),
            pltpu.VMEM((3, 3, 4, 2, 16, 128), BF16),
            pltpu.VMEM((4, 3, 2, 16, 128), BF16),
            pltpu.VMEM((3, 3, 2, 16, 128), BF16),
            pltpu.VMEM((4, 4, 16, 128), BF16),
            pltpu.VMEM((16, 4, 16, 128), BF16),
            dma((9,)), dma((9,)),
            dma((NCH,)), dma((NCH,)),
            dma((3,)), dma((3,)),
            dma((3, NCH)), dma((3, NCH)),
            dma((3,)), dma((3,)),
            dma((1,)), dma((1,)),
            pltpu.SemaphoreType.REGULAR, pltpu.SemaphoreType.REGULAR,
            dma((8,)), dma((8,)),
            dma((4,)), dma((4,)),
            dma((4, 3)), dma((4, 3)),
            dma((3, 3)), dma((3, 3)),
            dma((3, 3)), dma((3, 3)),
            dma((3, 3)), dma((3, 3)),
            dma((3, 8)), dma((3, 16)),
            dma((3, 3)), dma((3, 2)),
        ],
        compiler_params=pltpu.CompilerParams(
            collective_id=0, has_side_effects=True, vmem_limit_bytes=VMEM_LIMIT
        ),
        name="decoder_crps_step",
    )(*args)
    outs = pl.pallas_call(
        unpack,
        out_shape=(
            shape((PTS,), F32),
            shape((8, D), F32),
            shape((8, D), F32),
            shape((8, D), F32),
            shape((8, VARS), F32),
        ),
        in_specs=[vmem] * 2,
        out_specs=[vmem] * 5,
        compiler_params=pltpu.CompilerParams(vmem_limit_bytes=VMEM_LIMIT),
        name="unpack",
    )(crow, final)
    return outs


def solution(mesh):
    placed = (
        P("member", "band", None),
        P("member", "band", None),
        P("band", None),
        P(),
        P(None, "band"),
        P(),
        P(),
        P(),
        P(),
        P(),
    )
    return jax.shard_map(
        per_device,
        mesh=mesh,
        in_specs=placed,
        out_specs=(P("band"), P("band", None), P("band", None), P("band", None), P("band", None)),
        check_vma=False,
    )
```

```python
import jax
import jax.numpy as jnp
from jax import lax
from jax.experimental import pallas as pl
from jax.experimental.pallas import tpu as pltpu
from jax.sharding import PartitionSpec as P

HALO = 32
SMOOTH_SQ = 0.0625
MESH = pl.DeviceIdType.MESH
F32 = jnp.float32
BF16 = jnp.bfloat16

D = 512
NCH = 4
LEG = 3
PIECE_AT, PIECES = (0, 3, 5), (3, 2, 2)
SLOT_AT, SLOTS = (0, 2, 3), (2, 1, 1)
ORDER_Z = (8, 7, 9, 6, 10, 5, 11, 4, 12, 3, 13, 2, 14, 1, 15)
VMEM_LIMIT = 64 * 2**20 - 2**18
VARS = 100
PTS = 320
OWN = 128
ROWS = OWN + 2 * HALO
PACK = 256
TAIL = PTS - PACK
FOLD = 25


def dot(a, b, dims=((1,), (0,))):
    return lax.dot_general(a, b, (dims, ((), ())), preferred_element_type=F32)


def lanes_of(shape):
    return lax.broadcasted_iota(jnp.int32, shape, 1)


def rows_of(shape):
    return lax.broadcasted_iota(jnp.int32, shape, 0)


def pack_field(x):
    tail = x[PACK:]
    lane = lanes_of(tail.shape)
    inside = (lane >= VARS) & (lane < VARS + FOLD)
    parts = [jnp.where(inside, pltpu.roll(tail, VARS - FOLD * j, 1), 0.0) for j in range(4)]
    return x[:PACK] + jnp.concatenate(parts, axis=0)


def unpack_field(x):
    lane = lanes_of((TAIL, 128))
    tail = jnp.zeros((TAIL, 128), F32)
    for j in range(4):
        moved = pltpu.roll(x[TAIL * j : TAIL * (j + 1)], 128 - (VARS - FOLD * j), 1)
        tail = tail + jnp.where((lane >= FOLD * j) & (lane < FOLD * (j + 1)), moved, 0.0)
    main = jnp.where(lanes_of((PACK, 128)) < VARS, x, 0.0)
    return jnp.concatenate([main, tail], axis=0)


def kernel(
    mesh_hbm, grid_hbm, send_hbm, live_hbm, target_hbm, ws_hbm, wr_hbm, we_hbm, wo_hbm, gain_hbm,
    crow_z, final,
    mesh_ref, grid_ref, send_ref, live_ref, target_ref, ws_ref, wr_ref, we_ref, wo_ref, gain_ref,
    s_in, halo, held, wo, wpad, tpad, spad, onehot_t, slope_k, fields, crow,
    normed_t, agg_t, grid_t, mesh_t,
    part, part3, core_in, core_in3, summed, summed3, x_in1, x_in3, x_sum1, y_in1, y_in2, y_sum2, x_in2, slab, z_in,
    s_halo, r_halo, s_fz, r_fz, s_fy, r_fy, s_fzy, r_fzy, s_cy, r_cy, s_cz, r_cz,
    ok_z, ok_far, s_held, r_held, s_core, r_core, s_x1, r_x1, s_y1, r_y1, s_y2, r_y2, s_x2, r_x2, s_z, r_z, s_g, r_g,
):
    member = lax.axis_index("member")
    band = lax.axis_index("band")
    zh, y = member // 4, member % 4
    x, zl, c = band // 16, (band // 2) % 8, band % 2
    z = zh * 8 + zl

    def dev(z_, y_, x_, c_):
        return ((z_ // 8) * 4 + y_, x_ * 16 + (z_ % 8) * 2 + c_)

    def z_peer(k):
        return dev((z + k) % 16, y, x, c)

    def y_peer(k):
        return dev(z, (y + k) % 4, x, c)

    def x_peer(k):
        return dev(z, y, (x + k) % 4, c)

    sibling = dev(z, y, x, 1 - c)
    other = (member, (band + 2 * c - 1 + 64) % 64)
    far = zl == 7 * c
    near = jnp.logical_not(far)
    relay = zl == LEG + (7 - 2 * LEG) * c
    beyond = (member, (band + (2 * LEG + 1) * (2 * c - 1) + 64) % 64)
    to_relay = z_peer(LEG * (1 - 2 * c) + 16)

    def rcopy(src, dst, ss, rs, to):
        return pltpu.make_async_remote_copy(
            src_ref=src, dst_ref=dst, send_sem=ss, recv_sem=rs, device_id=to, device_id_type=MESH
        )

    barrier = pltpu.get_barrier_semaphore()

    def across(k):
        return dev((z + 8) % 16, (y + k) % 4, x, c)

    def greet(p):
        pl.semaphore_signal(barrier, inc=1, device_id=p, device_id_type=MESH)

    @pl.when(far)
    def _():
        greet(beyond)

    @pl.when(near)
    def _():
        greet(other)

    peers = [z_peer(k) for k in (4, 12, 3, 13, 2, 14, 1, 15)]
    peers += [y_peer(k) for k in (2, 1, 3)] + [x_peer(k) for k in (2, 1, 3)] + [sibling]
    for p in peers:
        greet(p)

    hbm = (mesh_hbm, ws_hbm, grid_hbm, wr_hbm, send_hbm, target_hbm, live_hbm, gain_hbm, wo_hbm, we_hbm)
    here = (mesh_ref, ws_ref, grid_ref, wr_ref, send_ref, target_ref, live_ref, gain_ref, wo_ref, we_ref)
    loads = [pltpu.make_async_copy(a, b, s_in.at[i]) for i, (a, b) in enumerate(zip(hbm, here))]
    for cp in loads:
        cp.start()

    sends, pending = [], {}

    def start(*copies):
        for cp in copies:
            cp.start()
            sends.append(cp)
            pending[id(cp)] = cp

    def arrive(*copies):
        for cp in copies:
            cp.wait_recv()
            del pending[id(cp)]

    def finish():
        arrive(*list(pending.values()))
        for cp in sends:
            cp.wait_send()

    loads[0].wait()
    loads[1].wait()
    sent_own = dot(mesh_ref[...], ws_ref[...])
    loads[2].wait()
    loads[3].wait()
    recv_rows = dot(grid_ref[...], wr_ref[...])
    pl.semaphore_wait(barrier, len(peers) + jnp.where(near, 1, 0) + jnp.where(relay, 1, 0))
    for k in (4, 12):
        pl.semaphore_signal(ok_z, inc=1, device_id=z_peer(k), device_id_type=MESH)

    facing = pl.multiple_of((OWN - HALO) * c, HALO)
    behind = pl.multiple_of((OWN - HALO) * (1 - c), HALO)
    tiles = [(i, j) for i in range(2) for j in range(4)]

    def tile(ref, n, base=0):
        i, j = tiles[n]
        return ref.at[pl.ds(pl.multiple_of(base + 16 * i, 16), 16), pl.ds(128 * j, 128)]

    direct, first_leg, second_leg = [], [], []
    for n in range(8):
        mine = tile(mesh_ref, n, facing)
        direct.append(rcopy(mine, tile(halo.at[0], n), s_halo.at[n], r_halo.at[n], other))
        first_leg.append(rcopy(mine, tile(held, n), s_halo.at[n], r_held.at[n], to_relay))
        second_leg.append(rcopy(tile(held, n), tile(halo.at[0], n), s_held.at[n], r_halo.at[n], beyond))

    @pl.when(far)
    def _():
        for cp in first_leg:
            cp.start()

    @pl.when(near)
    def _():
        for cp in direct:
            cp.start()

    close = rcopy(mesh_ref.at[pl.ds(behind, HALO)], halo.at[1], s_halo.at[8], r_halo.at[8], sibling)
    start(close)

    for cp in loads[4:]:
        cp.wait()
    wpad[...] = jnp.zeros(wpad.shape, F32)
    wpad[:VARS] = wo_ref[...].astype(F32)
    wo[...] = wpad[...].astype(BF16)
    tpad[...] = jnp.zeros(tpad.shape, F32)
    tpad[:VARS, :PTS] = target_ref[...].astype(F32)
    truth = pack_field(jnp.transpose(tpad[...])[:PTS])
    spad[...] = jnp.zeros(spad.shape, F32)
    spad[:3, :PTS] = send_ref[...].astype(F32)
    senders = jnp.transpose(spad[...])[:PTS].astype(jnp.int32)

    low_at = jnp.where(c == 0, OWN, OWN + HALO)
    high_at = jnp.where(c == 0, OWN + HALO, OWN)

    def moved(s):
        return jnp.where(s < HALO, s + low_at, jnp.where(s < HALO + OWN, s - HALO, s - (HALO + OWN) + high_at))

    index = moved(senders)
    index_t = moved(send_ref[...])
    for k in range(3):
        hit = rows_of((ROWS, PTS)) == index_t[k : k + 1, :]
        onehot_t[k] = jnp.where(hit, 1.0, 0.0).astype(BF16)
    live = live_ref[...]
    lane64 = lanes_of(live.shape)
    count = jnp.sum(jnp.where(lane64 == band, live, 0).astype(F32), axis=1, keepdims=True)
    total = jnp.sum(live.astype(F32), axis=1, keepdims=True)
    scale = 1.0 / (total * VARS)
    row = rows_of((PACK, 128))
    lane = lanes_of((PACK, 128))
    point = jnp.where(lane < VARS, row, PACK + row % TAIL)
    mask = jnp.where((lane < VARS + FOLD) & (point.astype(F32) < count), 1.0, 0.0)

    @pl.when(far)
    def _():
        pl.semaphore_wait(ok_z, 2)
        for k in (2, 1, 3):
            pl.semaphore_signal(ok_far, inc=1, device_id=y_peer(k), device_id_type=MESH)

    @pl.when(relay)
    def _():
        for n in range(8):
            first_leg[n].wait_recv()
            second_leg[n].start()

    arrive(close)
    for cp in direct:
        cp.wait_recv()
    polar = (band == 0) | (band == 63)
    outer = jnp.where(polar, 0.0, halo[0].astype(F32)).astype(BF16)
    edge_rows = jnp.concatenate([outer, halo[1]], axis=0)
    sent_edge = dot(edge_rows, ws_ref[...])
    sent = jnp.concatenate([sent_own, sent_edge], axis=0).astype(BF16)

    agg = jnp.zeros((PTS, D), F32)
    for k in range(3):
        hit = lanes_of((PTS, ROWS)) == index[:, k : k + 1]
        pre = dot(jnp.where(hit, 1.0, 0.0).astype(BF16), sent) + recv_rows
        sig = 0.5 * jnp.tanh(0.5 * pre) + 0.5
        act = pre * sig
        agg = agg + act
        slope_k[k] = sig + act * (1.0 - sig)
    agg_in = agg.astype(BF16)
    hidden = grid_ref[...].astype(F32) + dot(agg_in, we_ref[...])
    inv_rms = lax.rsqrt(jnp.mean(hidden * hidden, axis=1, keepdims=True) + 1e-05)
    gain = gain_ref[...]
    normed = (hidden * inv_rms * gain).astype(BF16)
    pred = dot(normed, wo[...], ((1,), (1,)))
    fields[0, 0] = pack_field(pred).astype(BF16)

    def rows(n):
        return pl.ds(PACK // NCH * n, PACK // NCH)

    fz = [
        rcopy(fields.at[0, 0, rows(n)], fields.at[1, 0, rows(n)], s_fz.at[n], r_fz.at[n], z_peer(8))
        for n in range(NCH)
    ]
    fy = [
        rcopy(fields.at[0, 0], fields.at[0, k], s_fy.at[k - 1], r_fy.at[k - 1], y_peer(k))
        for k in (1, 2, 3)
    ]
    fzy = [
        [
            rcopy(
                fields.at[1, 0, rows(n)], fields.at[1, k, rows(n)], s_fzy.at[k - 1, n], r_fzy.at[k - 1, n], y_peer(k)
            )
            for k in (1, 2, 3)
        ]
        for n in range(NCH)
    ]
    straight = [
        rcopy(fields.at[0, 0, rows(n)], fields.at[1, k, rows(n)], s_fzy.at[k - 1, n], r_fzy.at[k - 1, n], across(k))
        for n in range(NCH)
        for k in (2,)
    ]

    @pl.when(near)
    def _():
        pl.semaphore_wait(ok_z, 2)

    start(*fz)

    @pl.when(far)
    def _():
        pl.semaphore_wait(ok_far, 3)
        for cp in straight:
            cp.start()

    start(*fy)
    normed_t[...] = jnp.transpose(normed)
    agg_t[...] = jnp.transpose(agg_in)
    grid_t[...] = jnp.transpose(grid_ref[...])
    mesh_t[:, :OWN] = jnp.transpose(mesh_ref[...])
    mesh_t[:, OWN:] = jnp.transpose(edge_rows)

    own = fields[0, 0].astype(F32)
    error = own - truth
    error_sq = error * error + SMOOTH_SQ
    error_inv = lax.rsqrt(error_sq)
    pair_slope = jnp.zeros((PACK, 128), F32)
    spread = jnp.full((PACK, 128), 0.25, F32)

    def pair(h, k, pair_slope, spread):
        differ = own - fields[h, k].astype(F32)
        sq = differ * differ + SMOOTH_SQ
        inv = lax.rsqrt(sq)
        return pair_slope + differ * inv, spread + sq * inv

    for k in (1, 2, 3):
        arrive(fy[k - 1])
        pair_slope, spread = pair(0, k, pair_slope, spread)
    for n in range(NCH):
        arrive(fz[n])

        fzy[n][0].start()
        fzy[n][2].start()

        @pl.when(near)
        def _(n=n):
            fzy[n][1].start()

        for cp in fzy[n]:
            sends.append(cp)
            pending[id(cp)] = cp
    pair_slope, spread = pair(1, 0, pair_slope, spread)
    for k in (1, 2, 3):
        for n in range(NCH):
            arrive(fzy[n][k - 1])
        pair_slope, spread = pair(1, k, pair_slope, spread)

    field_grad = (error * error_inv * 0.125 - pair_slope * (1.0 / 56.0)) * (mask * scale)
    grad16 = unpack_field(field_grad).astype(BF16)


    def store_part(q, full):
        for t in range(2):
            halves = [full[:, 256 * t + 128 * i : 256 * t + 128 * (i + 1)].reshape(64, 8, 128) for i in range(2)]
            block = jnp.concatenate(halves, axis=1).astype(BF16).reshape(4, 4, 2, 2, 16, 128)
            for p in range(2):
                for cc in range(2):
                    part[cc, q, t, p] = block[:, :, p, cc]

    def store_head(full):
        bands = full.reshape(4, 4, 2, 2, 8, 128)
        for t in range(2):
            for p in range(2):
                for cc in range(2):
                    two = jnp.concatenate([bands[:, 2 * t, p, cc], bands[:, 2 * t + 1, p, cc]], axis=1)
                    part3[cc, p, t] = two.astype(BF16)

    core = [rcopy(part.at[1 - c, q], core_in.at[q], s_core.at[q], r_core.at[q], sibling) for q in range(3)]
    core.append(rcopy(part3.at[1 - c], core_in3, s_core.at[3], r_core.at[3], sibling))
    d_normed = dot(grad16, wo[...])
    store_head(dot(normed_t[...], grad16))
    start(core[3])
    gained = d_normed * gain
    mean = jnp.mean(gained * hidden, axis=1, keepdims=True)
    d_hidden = (inv_rms * gained - hidden * (inv_rms * inv_rms * inv_rms * mean)).astype(BF16)
    d_agg = dot(d_hidden, we_ref[...], ((1,), (1,)))
    store_part(2, dot(agg_t[...], d_hidden))
    start(core[2])
    d_recv = jnp.zeros((PTS, D), F32)
    d_sent = jnp.zeros((ROWS, D), F32)
    for k in range(3):
        d_pre = d_agg * slope_k[k]
        d_recv = d_recv + d_pre
        d_sent = d_sent + dot(onehot_t[k], d_pre.astype(BF16))
    store_part(1, dot(grid_t[...], d_recv.astype(BF16)))
    start(core[1])
    store_part(0, dot(mesh_t[...], d_sent.astype(BF16)))
    start(core[0])

    crps = (error_sq * error_inv * 0.125 - spread * (1.0 / 112.0)) * mask
    crps_hi = crps.astype(BF16)
    crps_lo = (crps - crps_hi.astype(F32)).astype(BF16)
    lane8 = lanes_of((8, 128))
    take_main = jnp.where(lane8 < VARS, 1.0, 0.0).astype(BF16)
    take_tail = jnp.where((lane8 >= VARS) & (lane8 < VARS + FOLD), 1.0, 0.0).astype(BF16)
    wide = ((1,), (1,))
    main = dot(take_main, crps_hi, wide) + dot(take_main, crps_lo, wide)
    tail = dot(take_tail, crps_hi, wide) + dot(take_tail, crps_lo, wide)
    tail = tail[:, :128] + tail[:, 128:]
    tail = tail + pltpu.roll(tail, 64, 1)
    crow[0, :, :256] = main
    crow[0, :, 256:] = tail
    cy = [rcopy(crow.at[0], crow.at[k], s_cy.at[k - 1], r_cy.at[k - 1], y_peer(k)) for k in (1, 2, 3)]
    start(*cy)

    def x1_copy(k, q):
        to = (x + k) % 4
        src = summed3.at[:, :, to] if q == 3 else summed.at[q, :, :, to, pl.ds(0, 2)]
        dst = x_in3.at[k - 1] if q == 3 else x_in1.at[q, k - 1]
        return rcopy(src, dst, s_x1.at[q, k - 1], r_x1.at[q, k - 1], x_peer(k))

    def y2_copy(k, q):
        to = (y + k) % 4
        src = summed.at[q, to % 2, to // 2, :, pl.ds(2, 2)]
        return rcopy(src, y_in2.at[q, k - 1], s_y2.at[q, k - 1], r_y2.at[q, k - 1], y_peer(k))

    x1 = [[x1_copy(k, q) for k in (1, 2, 3)] for q in range(4)]
    y2 = [[y2_copy(k, q) for k in (1, 2, 3)] for q in range(3)]

    def add(a, b):
        return (a.astype(F32) + b.astype(F32)).astype(BF16)

    for q in (3, 2, 1, 0):
        arrive(core[q])
        if q == 3:
            summed3[...] = add(part3[c], core_in3[...])
            start(*x1[q])
        else:
            summed[q] = add(part[c, q], core_in[q])
            for k in (1, 0, 2):
                start(x1[q][k], y2[q][k])

    arrive(*cy)
    crow_z[0] = (crow[0] + crow[1]) + (crow[2] + crow[3])
    cz = rcopy(crow_z.at[0], crow_z.at[1], s_cz.at[0], r_cz.at[0], z_peer(8))
    start(cz)

    def add4(a, b0, b1, b2):
        return ((a.astype(F32) + b0.astype(F32)) + (b1.astype(F32) + b2.astype(F32))).astype(BF16)

    def y1_copy(k, g):
        n = pl.ds(PIECE_AT[g], PIECES[g])
        return rcopy(x_sum1.at[(y + k) % 4, n], y_in1.at[k - 1, n], s_y1.at[g, k - 1], r_y1.at[g, k - 1], y_peer(k))

    def x2_copy(k, q):
        return rcopy(y_sum2.at[(x + k) % 4, q], x_in2.at[q, k - 1], s_x2.at[q, k - 1], r_x2.at[q, k - 1], x_peer(k))

    y1 = [[y1_copy(k, g) for k in (1, 2, 3)] for g in range(3)]
    x2 = [[x2_copy(k, q) for k in (1, 2, 3)] for q in range(3)]
    for q in (3, 2, 1, 0):
        arrive(*x1[q])
        if q == 3:
            head = add4(summed3[:, :, x], x_in3[0], x_in3[1], x_in3[2])
            for p in range(2):
                for t in range(2):
                    x_sum1[2 * p + t, 0] = head[p, t]
            continue
        g = 2 - q
        at = PIECE_AT[g] + PIECES[g] - 2
        body = add4(summed[q, :, :, x, 0:2], x_in1[q, 0], x_in1[q, 1], x_in1[q, 2])
        for p in range(2):
            for t in range(2):
                x_sum1[2 * p + t, at : at + 2] = body[t, p]
        start(y1[g][1], y1[g][0], y1[g][2])
        arrive(*y2[q])
        y_sum2[:, q] = add4(summed[q, y % 2, y // 2, :, 2:4], y_in2[q, 0], y_in2[q, 1], y_in2[q, 2])
        start(x2[q][1], x2[q][0], x2[q][2])

    away = (zl + y // 2) % 2
    owner = away == 0

    def z_copy(j, g, skip=0):
        k = 2 * j + away
        n = pl.ds(SLOT_AT[g] + skip, SLOTS[g] - skip)
        return rcopy(slab.at[((z + k) % 8) // 2, n], z_in.at[k, n], s_z.at[g, j], r_z.at[g, k], z_peer(k))

    def z_each(j, g, act):
        if g > 0:
            act(z_copy(j, g))
            return
        wanted = ((z + 2 * j + away) % 8) // 4 == y % 2

        @pl.when(wanted)
        def _():
            act(z_copy(j, 0))

        @pl.when(jnp.logical_not(wanted))
        def _():
            act(z_copy(j, 0, 1))

    def z_start(j, g):
        z_each(j, g, lambda cp: cp.start())

    def z_sent(j, g):
        z_each(j, g, lambda cp: cp.wait_send())

    def z_arrived(k, g, skip=0):
        n = pl.ds(SLOT_AT[g] + skip, SLOTS[g] - skip)
        rcopy(slab.at[0, n], z_in.at[k, n], s_z.at[g, 0], r_z.at[g, k], z_peer(8)).wait_recv()

    def z_sum(g, skip=0):
        n = pl.ds(SLOT_AT[g] + skip, SLOTS[g] - skip)
        acc = slab[zl // 2, n].astype(F32)
        for k in (1, 15, 2, 14, 3, 13, 4, 12, 5, 11, 6, 10, 7, 9, 8):
            z_arrived(k, g, skip)
            acc = acc + z_in[k, n].astype(F32)
        final[y % 2, n] = acc

    def g_copy(k, g):
        n = pl.ds(SLOT_AT[g], SLOTS[g])
        return rcopy(final.at[y % 2, n], final.at[y % 2, n], s_g.at[g, k - 1], r_g.at[g, y % 2], y_peer(k))

    for g in range(3):
        q = 2 - g
        lo, hi = SLOT_AT[g], SLOT_AT[g] + SLOTS[g]
        arrive(*y1[g])
        n = pl.ds(PIECE_AT[g], PIECES[g])
        done1 = add4(x_sum1[y, n], y_in1[0, n], y_in1[1, n], y_in1[2, n])
        if g == 0:
            for h in range(4):
                slab[h, 0] = done1[0]
        for h in range(2):
            slab[h, hi - 1] = done1[PIECES[g] - 2 + h]
        arrive(*x2[q])
        done2 = add4(y_sum2[x, q], x_in2[q, 0], x_in2[q, 1], x_in2[q, 2])
        for h in range(2):
            slab[2 + h, hi - 1] = done2[h]
        for j in (4, 3, 5, 2, 6, 1, 7):
            z_start(j, g)

        @pl.when(away == 1)
        def _(g=g):
            z_start(0, g)


    @pl.when(owner)
    def _():
        for g in range(3):
            if g > 0:
                z_sum(g)
            else:
                holds = zl // 4 == y % 2

                @pl.when(holds)
                def _():
                    z_sum(0)

                @pl.when(jnp.logical_not(holds))
                def _():
                    final[y % 2, 0] = jnp.zeros((16, 128), F32)
                    z_sum(0, 1)

            for k in (2, 1, 3):
                g_copy(k, g).start()

    arrive(cz)
    for t in range(2):

        @pl.when(jnp.logical_not(owner & (y % 2 == t)))
        def _(t=t):
            for g in range(3):
                n = pl.ds(SLOT_AT[g], SLOTS[g])
                rcopy(final.at[t, n], final.at[t, n], s_g.at[g, 0], r_g.at[g, t], z_peer(8)).wait_recv()

    @pl.when(owner)
    def _():
        for g in range(3):
            for k in (1, 2, 3):
                g_copy(k, g).wait_send()

    @pl.when(away == 1)
    def _():
        for g in range(3):
            z_sent(0, g)

    for g in range(3):
        for j in range(1, 8):
            z_sent(j, g)
    for cp in direct:
        cp.wait_send()

    @pl.when(relay)
    def _():
        for cp in second_leg:
            cp.wait_send()

    finish()


def unpack(crow_ref, final_ref, crps_out, gs_out, gr_out, ge_out, go_out):
    zl = (lax.axis_index("band") // 2) % 8
    crps_out[...] = (crow_ref[0] + crow_ref[1])[0, :PTS]
    for q, out in ((0, gs_out), (1, gr_out), (2, ge_out)):
        for t in range(2):
            got = final_ref[t, 3 - q]
            out[:, 256 * t : 256 * t + 128] = got[:8]
            out[:, 256 * t + 128 : 256 * t + 256] = got[8:]
    got = final_ref[zl // 4, 0]
    go_out[...] = jnp.where((zl // 2) % 2 == 0, got[:8, :VARS], got[8:, :VARS])


def per_device(mesh_latent, grid_latent, senders, live_points, target, w_send, w_recv, w_edge, w_out, gain):
    vmem = pl.BlockSpec(memory_space=pltpu.VMEM)
    dma = pltpu.SemaphoreType.DMA
    shape = jax.ShapeDtypeStruct
    args = (
        mesh_latent[0], grid_latent[0], senders.T, live_points.reshape(1, -1), target,
        w_send, w_recv, w_edge, w_out.T, gain.reshape(1, -1),
    )
    crow, final = pl.pallas_call(
        kernel,
        out_shape=(shape((2, 8, 384), F32), shape((2, 4, 16, 128), F32)),
        in_specs=[pl.BlockSpec(memory_space=pltpu.HBM)] * 10,
        out_specs=[vmem] * 2,
        scratch_shapes=[pltpu.VMEM(a.shape, a.dtype) for a in args]
        + [
            dma((10,)),
            pltpu.VMEM((2, HALO, D), BF16),
            pltpu.VMEM((HALO, D), BF16),
            pltpu.VMEM((128, D), BF16),
            pltpu.VMEM((128, D), F32),
            pltpu.VMEM((128, 384), F32),
            pltpu.VMEM((128, 384), F32),
            pltpu.VMEM((3, ROWS, PTS), BF16),
            pltpu.VMEM((3, PTS, D), F32),
            pltpu.VMEM((2, 4, PACK, 128), BF16),
            pltpu.VMEM((4, 8, 384), F32),
            pltpu.VMEM((D, PTS), BF16),
            pltpu.VMEM((D, PTS), BF16),
            pltpu.VMEM((D, PTS), BF16),
            pltpu.VMEM((D, ROWS), BF16),
            pltpu.VMEM((2, 3, 2, 2, 4, 4, 16, 128), BF16),
            pltpu.VMEM((2, 2, 2, 4, 16, 128), BF16),
            pltpu.VMEM((3, 2, 2, 4, 4, 16, 128), BF16),
            pltpu.VMEM((2, 2, 4, 16, 128), BF16),
            pltpu.VMEM((3, 2, 2, 4, 4, 16, 128), BF16),
            pltpu.VMEM((2, 2, 4, 16, 128), BF16),
            pltpu.VMEM((3, 3, 2, 2, 2, 16, 128), BF16),
            pltpu.VMEM((3, 2, 2, 16, 128), BF16),
            pltpu.VMEM((4, 7, 16, 128), BF16),
            pltpu.VMEM((3, 7, 16, 128), BF16),
            pltpu.VMEM((3, 3, 4, 2, 16, 128), BF16),
            pltpu.VMEM((4, 3, 2, 16, 128), BF16),
            pltpu.VMEM((3, 3, 2, 16, 128), BF16),
            pltpu.VMEM((4, 4, 16, 128), BF16),
            pltpu.VMEM((16, 4, 16, 128), BF16),
            dma((9,)), dma((9,)),
            dma((NCH,)), dma((NCH,)),
            dma((3,)), dma((3,)),
            dma((3, NCH)), dma((3, NCH)),
            dma((3,)), dma((3,)),
            dma((1,)), dma((1,)),
            pltpu.SemaphoreType.REGULAR, pltpu.SemaphoreType.REGULAR,
            dma((8,)), dma((8,)),
            dma((4,)), dma((4,)),
            dma((4, 3)), dma((4, 3)),
            dma((3, 3)), dma((3, 3)),
            dma((3, 3)), dma((3, 3)),
            dma((3, 3)), dma((3, 3)),
            dma((3, 8)), dma((3, 16)),
            dma((3, 3)), dma((3, 2)),
        ],
        compiler_params=pltpu.CompilerParams(
            collective_id=0, has_side_effects=True, vmem_limit_bytes=VMEM_LIMIT
        ),
        name="decoder_crps_step",
    )(*args)
    outs = pl.pallas_call(
        unpack,
        out_shape=(
            shape((PTS,), F32),
            shape((8, D), F32),
            shape((8, D), F32),
            shape((8, D), F32),
            shape((8, VARS), F32),
        ),
        in_specs=[vmem] * 2,
        out_specs=[vmem] * 5,
        compiler_params=pltpu.CompilerParams(vmem_limit_bytes=VMEM_LIMIT),
        name="unpack",
    )(crow, final)
    return outs


def solution(mesh):
    placed = (
        P("member", "band", None),
        P("member", "band", None),
        P("band", None),
        P(),
        P(None, "band"),
        P(),
        P(),
        P(),
        P(),
        P(),
    )
    return jax.shard_map(
        per_device,
        mesh=mesh,
        in_specs=placed,
        out_specs=(P("band"), P("band", None), P("band", None), P("band", None), P("band", None)),
        check_vma=False,
    )
```
